256 devices in a mesh: dp: 64 (over y, z, core), tensor: 4 (over x).
Axes of the slice: x: 4, y: 4, z: 8, core: 2. Of those that a mesh axis runs over, the one named last changes fastest.
Arguments:
- layer_input: bfloat16 [16384, 4096], P(('dp', 'tensor')), may hold values from -6 to 6
- pre_grad: bfloat16 [16384, 5120], P('dp', 'tensor'), may hold values from -6 to 6
- weight_in: bfloat16 [4096, 5120], P(None, 'tensor'), may hold values from -0.09375 to 0.09375
- coeff_prev: float32 [5120, 32], P('tensor'), may hold values from -6 to 6
Outputs:
- input_grad: bfloat16 [16384, 4096], P(('dp', 'tensor'))
- factor_basis: float32 [4096, 32], P('tensor')
- coeff_next: float32 [5120, 32], P('tensor')
The draws below stay inside these ranges and needn't reach their ends.
All inputs are finite; a program needn't handle non-finite values.
Results may differ from the reference program's by a relative error of at most 0.013.
Values may be sent and summed in bfloat16 or wider, within the bound.
A program may use at most 128 MiB of HBM per device.

```python
import math
import jax
import jax.numpy as jnp
from jax import lax

D = 4096
FF = 5120
RANK = 32
TOKENS = 16384
N_TENSOR = 4


def levels(rng, dims, split, least, top_value):
    def one(position, shards_of):
        heights = jax.random.uniform(jax.random.fold_in(jax.random.fold_in(rng, 6), position), (shards_of,), jnp.float32, least / len(split), top_value / len(split))
        return jnp.repeat(jnp.exp(heights), dims[position] // shards_of).reshape((-1,) + (1,) * (len(dims) - position - 1))

    level = one(*split[0])
    for cut in split[1:]:
        level = level * one(*cut)
    return level


def gaussian(stream_key, shape, scale, most, split=(), held_as=jnp.bfloat16):
    level = levels(stream_key, shape, split, -0.22, 0.18) if split else 1.0
    entries = jax.random.normal(stream_key, shape, jnp.float32) * scale * level
    return jnp.minimum(jnp.maximum(entries, -most), most).astype(held_as)


def setup_inputs(seed: int = 0) -> dict:
    splits = jax.random.split(jax.random.key(seed), 5)
    layer_input = gaussian(splits[0], (TOKENS, D), 1.0, 6.0, ((0, 256),))
    pre_grad = gaussian(splits[1], (TOKENS, FF), 1.0, 6.0, ((0, 64), (1, 4)))
    weight_in = gaussian(splits[2], (D, FF), D ** -0.5, 0.09375, ((1, 4),))
    coeff_prev = gaussian(splits[3], (FF, RANK), 1.0, 6.0, ((0, 4),), jnp.float32)
    return {"layer_input": layer_input, "pre_grad": pre_grad, "weight_in": weight_in, "coeff_prev": coeff_prev}


def orthonormal(factor, gram_matrix):
    cholesky_factor = jnp.linalg.cholesky(gram_matrix)
    solved = jax.scipy.linalg.solve_triangular(cholesky_factor, factor.T, lower=True)
    return solved.T

def reference(layer_input, pre_grad, weight_in, coeff_prev):
    loss_scale = 1.0 / math.sqrt(TOKENS)
    grad = lax.dot_general(layer_input.astype(jnp.float32), pre_grad.astype(jnp.float32), (((0,), (0,)), ((), ())), preferred_element_type=jnp.float32) * loss_scale
    block_width = FF // N_TENSOR
    summed = jnp.zeros((TOKENS, D), jnp.float32)
    for block in range(N_TENSOR):
        grad_block = pre_grad[:, block * block_width:(block + 1) * block_width]
        weight_block = weight_in[:, block * block_width:(block + 1) * block_width]
        partial_term = lax.dot_general(grad_block.astype(jnp.float32), weight_block.astype(jnp.float32), (((1,), (1,)), ((), ())), preferred_element_type=jnp.float32)
        rounded = lax.optimization_barrier(partial_term.astype(jnp.bfloat16))
        summed = summed + rounded.astype(jnp.float32)
    input_grad = summed.astype(jnp.bfloat16)
    factor = jnp.dot(grad.astype(jnp.float32), coeff_prev.astype(jnp.float32), precision=lax.Precision.HIGHEST, preferred_element_type=jnp.float32)
    gram_matrix = jnp.dot(factor.T.astype(jnp.float32), factor.astype(jnp.float32), precision=lax.Precision.HIGHEST, preferred_element_type=jnp.float32)
    factor_basis = orthonormal(factor, gram_matrix)
    coeff_next = lax.dot_general(grad.astype(jnp.float32), factor_basis.astype(jnp.float32), (((0,), (0,)), ((), ())), precision=lax.Precision.HIGHEST, preferred_element_type=jnp.float32)
    return (input_grad, factor_basis, coeff_next)
```

```python
import functools
import math

import jax
import jax.numpy as jnp
from jax import lax
from jax.experimental import pallas as pl
from jax.experimental.pallas import tpu as pltpu
from jax.sharding import PartitionSpec as P

MESH = pl.DeviceIdType.MESH
HIGH = lax.Precision.HIGHEST
F32 = jnp.float32
BF16 = jnp.bfloat16
NN = (((1,), (0,)), ((), ()))
NT = (((1,), (1,)), ((), ()))
R = 32
NY, NZ = 4, 8


def split3(a):
    hi = a.astype(BF16)
    rest = a - hi.astype(F32)
    mid = rest.astype(BF16)
    low = (rest - mid.astype(F32)).astype(BF16)
    return jnp.concatenate([hi, mid, low], axis=0)


def fdot(a, b, dims):
    r = lax.dot_general(split3(a), b, dims, preferred_element_type=F32)
    return r[0:R] + r[R : 2 * R] + r[2 * R : 3 * R]


def inverse_cholesky(gram):
    n = gram.shape[0]
    row = lax.broadcasted_iota(jnp.int32, (n, n), 0)
    col = lax.broadcasted_iota(jnp.int32, (n, n), 1)
    eye = jnp.where(row == col, 1.0, 0.0).astype(F32)
    m = jnp.concatenate([gram, eye], axis=1)
    below = lax.broadcasted_iota(jnp.int32, (n, 1), 0)
    diag = jnp.zeros((n, 1), F32)
    for j in range(n):
        pivot = m[j : j + 1, j : j + 1]
        column = m[:, j : j + 1]
        diag = jnp.where(below == j, pivot, diag)
        factor = jnp.where(below > j, column / pivot, 0.0)
        m = m - factor * m[j : j + 1, :]
    return m[:, n : 2 * n] / jnp.sqrt(diag)


def far_offset(j, half):
    return half + lax.div(j + 1, 2) * (1 - 2 * lax.rem(j, 2))


def kernel(
    scale,
    x_ref, g_ref, w_ref, q_ref,
    ig_ref, basis_ref, coeff_ref,
    xv, gv, qv, wv, xs, yr, fp, r2, f3, zr, cp, r4, c3,
    igp, dira, dirb, rela, relb, suma, sumb, fina, finb, igo, bas, cof,
    lsem, wsem, osem, ysem_s, ysem_r, xsem_s, xsem_r, zsem_s, zsem_r,
    rsem, isem_s, isem_r,
):
    d = lax.axis_index("dp")
    t = lax.axis_index("tensor")
    chip = lax.div(d, 2)
    core = lax.rem(d, 2)
    cy, cz = lax.div(chip, NZ), lax.rem(chip, NZ)
    nt = 4
    tok = xv.shape[0]
    share = xs.shape[2]
    half = igp.shape[1] // 2
    left, right, across = lax.rem(t + 3, nt), lax.rem(t + 1, nt), lax.rem(t + 2, nt)

    def other_chips(fn):
        def body(k, carry):
            qy = lax.rem(cy + far_offset(lax.rem(k, NY), NY // 2), NY)
            qz = lax.rem(cz + far_offset(lax.div(k, NY), NZ // 2), NZ)
            fn(qy * NZ + qz)
            return carry

        lax.fori_loop(0, NY * NZ - 1, body, 0)

    loads = [
        pltpu.make_async_copy(q_ref, qv, lsem.at[0]),
        pltpu.make_async_copy(g_ref, gv, lsem.at[1]),
        pltpu.make_async_copy(x_ref, xv, lsem.at[2]),
        pltpu.make_async_copy(
            x_ref.at[:, pl.ds(pl.multiple_of(t * share, share), share)], xs.at[t], lsem.at[3]
        ),
    ]
    for c in loads:
        c.start()
    nb = wsem.shape[0]
    wb = wv.shape[0] // nb

    def w_copy(b):
        rows = pl.ds(pl.multiple_of(b * wb, wb), wb)
        return pltpu.make_async_copy(w_ref.at[rows], wv.at[rows], wsem.at[b])

    for b in range(nb):
        w_copy(b).start()

    bar = pltpu.get_barrier_semaphore()

    def greet(dp, tt):
        pl.semaphore_signal(bar, inc=1, device_id=(dp, tt), device_id_type=MESH)

    def greet_chip(q):
        greet(2 * q, t)
        greet(2 * q + 1, t)

    other_chips(greet_chip)
    greet(2 * chip + 1 - core, t)
    for k in range(1, nt):
        greet(d, lax.rem(t + k, nt))

    loads[0].wait()
    loads[1].wait()
    yr[t] = fdot(qv[...], gv[...], NT)

    def ig_block(b, carry):
        w_copy(b).wait()
        rows = pl.ds(pl.multiple_of(b * wb, wb), wb)
        igp[:, rows] = lax.dot_general(gv[...], wv[rows, :], NT, preferred_element_type=F32).astype(BF16)
        return carry

    lax.fori_loop(0, nb, ig_block, 0)
    loads[2].wait()

    pl.semaphore_wait(bar, 2 * NY * NZ - 1 + nt - 1)

    ycopies, xcopies = [], []
    for k in range(1, nt):
        to = lax.rem(t + k, nt)
        ycopies.append(pltpu.make_async_remote_copy(
            src_ref=yr.at[t], dst_ref=yr.at[t], send_sem=ysem_s.at[k - 1], recv_sem=ysem_r.at[k - 1],
            device_id=(d, to), device_id_type=MESH))
        xcopies.append(pltpu.make_async_remote_copy(
            src_ref=xv.at[:, pl.ds(pl.multiple_of(to * share, share), share)], dst_ref=xs.at[t],
            send_sem=xsem_s.at[k - 1], recv_sem=xsem_r.at[k - 1],
            device_id=(d, to), device_id_type=MESH))
    for c in ycopies:
        c.start()
    for c in xcopies:
        c.start()
    for c in ycopies:
        c.wait_recv()
    yt = (yr[0] + yr[1]) + (yr[2] + yr[3])
    for c in xcopies:
        c.wait_recv()
    loads[3].wait()

    xsl = xs[...].reshape(nt * tok, share)
    part = fdot(yt, xsl, NN) * scale
    ncol = share // 128
    for i in range(R // 8):
        for j in range(ncol):
            fp[i * ncol + j] = part[8 * i : 8 * i + 8, 128 * j : 128 * j + 128]

    def wait_tiles(ref, n, sem):
        view = ref.at[pl.ds(0, n)]
        pltpu.make_async_copy(view, view, sem).wait()

    def tile_copy(src, dst, dp, s, r):
        return pltpu.make_async_remote_copy(
            src_ref=src, dst_ref=dst, send_sem=rsem.at[s], recv_sem=rsem.at[r],
            device_id=(dp, t), device_id_type=MESH)

    def slot(to):
        return lax.rem(d - to + 127, 64)

    other_chips(lambda q: tile_copy(fp.at[q], r2.at[slot(2 * q)], 2 * q, 0, 1).start())

    @pl.when(core == 1)
    def _():
        tile_copy(fp.at[chip], r2.at[slot(2 * chip)], 2 * chip, 0, 1).start()

    def rows_of(o):
        return pl.ds(pl.multiple_of(o * tok, tok), tok)

    def ig_copy(n, src, dst, to):
        return pltpu.make_async_remote_copy(
            src_ref=src, dst_ref=dst, send_sem=isem_s.at[n], recv_sem=isem_r.at[n],
            device_id=(d, to), device_id_type=MESH)

    ca, cb = pl.ds(0, half), pl.ds(half, half)
    c_rela = ig_copy(0, igp.at[rows_of(across), ca], rela, left)
    c_relb = ig_copy(1, igp.at[rows_of(across), cb], relb, right)
    c_dira = ig_copy(2, igp.at[rows_of(right), ca], dira, right)
    c_dirb = ig_copy(3, igp.at[rows_of(left), cb], dirb, left)
    for c in (c_rela, c_relb, c_dira, c_dirb):
        c.start()

    @pl.when(core == 0)
    def _():
        r2[63] = fp[chip]
        wait_tiles(r2, 63, rsem.at[1])
        f3[chip] = jnp.sum(r2[...], axis=0)

        def to_chip(q):
            for c in range(2):
                tile_copy(f3.at[chip], f3.at[chip], 2 * q + c, 2, 3).start()

        other_chips(to_chip)
        tile_copy(f3.at[chip], f3.at[chip], 2 * chip + 1, 2, 3).start()

    c_rela.wait_recv()
    suma[...] = (rela[...].astype(F32) + igp[rows_of(left), ca].astype(F32)).astype(BF16)
    c_fina = ig_copy(4, suma, fina, left)
    c_fina.start()
    c_relb.wait_recv()
    sumb[...] = (relb[...].astype(F32) + igp[rows_of(right), cb].astype(F32)).astype(BF16)
    c_finb = ig_copy(5, sumb, finb, right)
    c_finb.start()

    @pl.when(core == 0)
    def _():
        wait_tiles(f3, 31, rsem.at[3])

    @pl.when(core == 1)
    def _():
        wait_tiles(f3, 32, rsem.at[3])

    ft = jnp.concatenate(
        [jnp.concatenate([f3[i * ncol + j] for j in range(ncol)], axis=1) for i in range(R // 8)], axis=0
    )

    zw = nt * tok
    zr[t, :, 0:zw] = fdot(ft, xsl, NT) * scale
    zr[t, :, zw : zw + R] = lax.dot_general(ft, ft, NT, precision=HIGH, preferred_element_type=F32)
    zcopies = []
    for k in range(1, nt):
        zcopies.append(pltpu.make_async_remote_copy(
            src_ref=zr.at[t], dst_ref=zr.at[t], send_sem=zsem_s.at[k - 1], recv_sem=zsem_r.at[k - 1],
            device_id=(d, lax.rem(t + k, nt)), device_id_type=MESH))
    for c in zcopies:
        c.start()
    for c in zcopies:
        c.wait_recv()
    zt = (zr[0, :, 0:zw] + zr[1, :, 0:zw]) + (zr[2, :, 0:zw] + zr[3, :, 0:zw])
    gs = slice(zw, zw + R)
    gram = (zr[0, :, gs] + zr[1, :, gs]) + (zr[2, :, gs] + zr[3, :, gs])

    cpart = fdot(zt, gv[...], NN)
    ncc = cpart.shape[1] // 128
    nct = R // 8 * ncc
    for i in range(R // 8):
        for j in range(ncc):
            cp[i * ncc + j] = cpart[8 * i : 8 * i + 8, 128 * j : 128 * j + 128]
    other_chips(lambda q: tile_copy(cp.at[q], r4.at[slot(2 * q)], 2 * q, 4, 5).start())

    @pl.when(core == 1)
    def _():
        tile_copy(cp.at[chip], r4.at[slot(2 * chip)], 2 * chip, 4, 5).start()

    @pl.when(core == 0)
    def _():
        r4[63] = cp[chip]

    for e in range(nct - 32):
        to = 8 * e + 1

        @pl.when(d != to)
        def _():
            tile_copy(cp.at[32 + e], r4.at[slot(to)], to, 4, 5).start()

        @pl.when(d == to)
        def _():
            r4[63] = cp[32 + e]

    c_dira.wait_recv()
    c_fina.wait_recv()
    igo[:, ca] = (igp[rows_of(t), ca].astype(F32) + dira[...].astype(F32) + fina[...].astype(F32)).astype(BF16)
    c_dirb.wait_recv()
    c_finb.wait_recv()
    igo[:, cb] = (igp[rows_of(t), cb].astype(F32) + dirb[...].astype(F32) + finb[...].astype(F32)).astype(BF16)
    o_ig = pltpu.make_async_copy(igo, ig_ref, osem.at[0])
    o_ig.start()

    linv = inverse_cholesky(gram)
    bas[...] = lax.dot_general(linv, ft, NN, precision=HIGH, preferred_element_type=F32)
    o_bas = pltpu.make_async_copy(bas, basis_ref, osem.at[1])
    o_bas.start()

    owner = jnp.logical_or(core == 0, lax.rem(chip, 4) == 0)
    mine = chip * (1 - core) + (32 + lax.div(chip, 4)) * core

    @pl.when(owner)
    def _():
        wait_tiles(r4, 63, rsem.at[5])
        c3[mine] = jnp.sum(r4[...], axis=0)

        def to_chip(q):
            for c in range(2):
                tile_copy(c3.at[mine], c3.at[mine], 2 * q + c, 6, 7).start()

        other_chips(to_chip)
        tile_copy(c3.at[mine], c3.at[mine], 2 * chip + 1 - core, 6, 7).start()
        wait_tiles(c3, nct - 1, rsem.at[7])

    @pl.when(jnp.logical_not(owner))
    def _():
        wait_tiles(c3, nct, rsem.at[7])

    ct = jnp.concatenate(
        [jnp.concatenate([c3[i * ncc + j] for j in range(ncc)], axis=1) for i in range(R // 8)], axis=0
    )
    cof[...] = lax.dot_general(linv, ct, NN, precision=HIGH, preferred_element_type=F32)
    o_cof = pltpu.make_async_copy(cof, coeff_ref, osem.at[2])
    o_cof.start()

    for c in ycopies + xcopies + zcopies + [c_rela, c_relb, c_dira, c_dirb, c_fina, c_finb]:
        c.wait_send()

    @pl.when(core == 0)
    def _():
        wait_tiles(r2, 31, rsem.at[0])
        wait_tiles(r2, 63, rsem.at[2])

    @pl.when(core == 1)
    def _():
        wait_tiles(r2, 32, rsem.at[0])

    @pl.when(owner)
    def _():
        wait_tiles(r4, nct - 1, rsem.at[4])
        wait_tiles(r4, 63, rsem.at[6])

    @pl.when(jnp.logical_not(owner))
    def _():
        wait_tiles(r4, nct, rsem.at[4])

    o_ig.wait()
    o_bas.wait()
    o_cof.wait()


def local(layer_input, pre_grad, weight_in, coeff_prev):
    rows = pre_grad.shape[0]
    scale = 1.0 / math.sqrt(rows * lax.axis_size("dp"))
    tok, width = layer_input.shape
    nt = lax.axis_size("tensor")
    hid = pre_grad.shape[1]
    share = width // nt
    half = width // 2
    nb = 8
    dma = pltpu.SemaphoreType.DMA
    vm = pltpu.VMEM
    any_spec = pl.BlockSpec(memory_space=pl.ANY)
    ig, basis, coeff = pl.pallas_call(
        functools.partial(kernel, scale),
        out_shape=(
            jax.ShapeDtypeStruct((tok, width), BF16),
            jax.ShapeDtypeStruct((R, share), F32),
            jax.ShapeDtypeStruct((R, hid), F32),
        ),
        in_specs=[any_spec] * 4,
        out_specs=(any_spec,) * 3,
        scratch_shapes=[
            vm((tok, width), BF16), vm((rows, hid), BF16), vm((R, hid), F32), vm((width, hid), BF16),
            vm((nt, tok, share), BF16), vm((nt, R, rows), F32),
            vm((32, 8, 128), F32), vm((64, 8, 128), F32), vm((32, 8, 128), F32),
            vm((nt, R, rows + 128), F32),
            vm((40, 8, 128), F32), vm((64, 8, 128), F32), vm((40, 8, 128), F32),
            vm((rows, width), BF16),
            *[vm((tok, half), BF16)] * 8,
            vm((tok, width), BF16), vm((R, share), F32), vm((R, hid), F32),
            dma((4,)), dma((nb,)), dma((3,)),
            dma((3,)), dma((3,)), dma((3,)), dma((3,)), dma((3,)), dma((3,)),
            dma((8,)), dma((6,)), dma((6,)),
        ],
        compiler_params=pltpu.CompilerParams(
            collective_id=0, has_side_effects=True, vmem_limit_bytes=48 * 2**20
        ),
    )(layer_input, pre_grad, weight_in, coeff_prev.T)
    return ig, basis.T, coeff.T


def solution(mesh):
    return jax.shard_map(
        local,
        mesh=mesh,
        in_specs=(
            P(("dp", "tensor"), None),
            P("dp", "tensor"),
            P(None, "tensor"),
            P("tensor", None),
        ),
        out_specs=(P(("dp", "tensor"), None), P("tensor", None), P("tensor", None)),
        check_vma=False,
    )
```

```python
import functools
import math

import jax
import jax.numpy as jnp
from jax import lax
from jax.experimental import pallas as pl
from jax.experimental.pallas import tpu as pltpu
from jax.sharding import PartitionSpec as P

MESH = pl.DeviceIdType.MESH
HIGH = lax.Precision.HIGHEST
F32 = jnp.float32
BF16 = jnp.bfloat16
NN = (((1,), (0,)), ((), ()))
NT = (((1,), (1,)), ((), ()))
R = 32
NY, NZ = 4, 8


def split3(a):
    hi = a.astype(BF16)
    rest = a - hi.astype(F32)
    mid = rest.astype(BF16)
    low = (rest - mid.astype(F32)).astype(BF16)
    return jnp.concatenate([hi, mid, low], axis=0)


def fdot(a, b, dims):
    r = lax.dot_general(split3(a), b, dims, preferred_element_type=F32)
    return r[0:R] + r[R : 2 * R] + r[2 * R : 3 * R]


def inverse_cholesky(gram):
    n = gram.shape[0]
    row = lax.broadcasted_iota(jnp.int32, (n, n), 0)
    col = lax.broadcasted_iota(jnp.int32, (n, n), 1)
    eye = jnp.where(row == col, 1.0, 0.0).astype(F32)
    m = jnp.concatenate([gram, eye], axis=1)
    below = lax.broadcasted_iota(jnp.int32, (n, 1), 0)
    diag = jnp.zeros((n, 1), F32)
    for j in range(n):
        pivot = m[j : j + 1, j : j + 1]
        column = m[:, j : j + 1]
        diag = jnp.where(below == j, pivot, diag)
        factor = jnp.where(below > j, column / pivot, 0.0)
        m = m - factor * m[j : j + 1, :]
    return m[:, n : 2 * n] / jnp.sqrt(diag)


def far_offset(j, half):
    return half + lax.div(j + 1, 2) * (1 - 2 * lax.rem(j, 2))


def kernel(
    scale,
    x_ref, g_ref, w_ref, q_ref,
    igo, bas, cof,
    xv, gv, qv, wv, xs, yr, fp, r2, f3, zr, cp, r4, c3,
    igp, dira, dirb, rela, relb, suma, sumb, fina, finb,
    lsem, wsem, ysem_s, ysem_r, xsem_s, xsem_r, zsem_s, zsem_r,
    rsem, isem_s, isem_r,
):
    d = lax.axis_index("dp")
    t = lax.axis_index("tensor")
    chip = lax.div(d, 2)
    core = lax.rem(d, 2)
    cy, cz = lax.div(chip, NZ), lax.rem(chip, NZ)
    nt = 4
    tok = xv.shape[0]
    share = xs.shape[2]
    half = igp.shape[1] // 2
    left, right, across = lax.rem(t + 3, nt), lax.rem(t + 1, nt), lax.rem(t + 2, nt)

    def other_chips(fn):
        def body(k, carry):
            qy = lax.rem(cy + far_offset(lax.rem(k, NY), NY // 2), NY)
            qz = lax.rem(cz + far_offset(lax.div(k, NY), NZ // 2), NZ)
            fn(qy * NZ + qz)
            return carry

        lax.fori_loop(0, NY * NZ - 1, body, 0)

    bar = pltpu.get_barrier_semaphore()

    def greet(dp, tt):
        pl.semaphore_signal(bar, inc=1, device_id=(dp, tt), device_id_type=MESH)

    def greet_chip(q):
        greet(2 * q, t)
        greet(2 * q + 1, t)

    other_chips(greet_chip)
    greet(2 * chip + 1 - core, t)
    for k in range(1, nt):
        greet(d, lax.rem(t + k, nt))

    loads = [
        pltpu.make_async_copy(q_ref, qv, lsem.at[0]),
        pltpu.make_async_copy(g_ref, gv, lsem.at[1]),
        pltpu.make_async_copy(x_ref, xv, lsem.at[2]),
        pltpu.make_async_copy(
            x_ref.at[:, pl.ds(pl.multiple_of(t * share, share), share)], xs.at[t], lsem.at[3]
        ),
    ]
    for c in loads:
        c.start()
    nb = wsem.shape[0]
    wb = wv.shape[0] // nb

    def w_copy(b):
        rows = pl.ds(pl.multiple_of(b * wb, wb), wb)
        return pltpu.make_async_copy(w_ref.at[rows], wv.at[rows], wsem.at[b])

    for b in range(nb):
        w_copy(b).start()

    loads[0].wait()
    loads[1].wait()
    yr[t] = fdot(qv[...], gv[...], NT)

    loads[2].wait()

    pl.semaphore_wait(bar, 2 * NY * NZ - 1 + nt - 1)

    ycopies, xcopies = [], []
    for k in range(1, nt):
        to = lax.rem(t + k, nt)
        ycopies.append(pltpu.make_async_remote_copy(
            src_ref=yr.at[t], dst_ref=yr.at[t], send_sem=ysem_s.at[k - 1], recv_sem=ysem_r.at[k - 1],
            device_id=(d, to), device_id_type=MESH))
        xcopies.append(pltpu.make_async_remote_copy(
            src_ref=xv.at[:, pl.ds(pl.multiple_of(to * share, share), share)], dst_ref=xs.at[t],
            send_sem=xsem_s.at[k - 1], recv_sem=xsem_r.at[k - 1],
            device_id=(d, to), device_id_type=MESH))
    for c in ycopies:
        c.start()
    for c in xcopies:
        c.start()

    def ig_block(b, carry):
        w_copy(b).wait()
        rows = pl.ds(pl.multiple_of(b * wb, wb), wb)
        igp[:, rows] = lax.dot_general(gv[...], wv[rows, :], NT, preferred_element_type=F32).astype(BF16)
        return carry

    lax.fori_loop(0, nb, ig_block, 0)

    for c in ycopies:
        c.wait_recv()
    yt = (yr[0] + yr[1]) + (yr[2] + yr[3])
    for c in xcopies:
        c.wait_recv()
    loads[3].wait()

    xsl = xs[...].reshape(nt * tok, share)
    part = fdot(yt, xsl, NN) * scale
    ncol = share // 128
    for i in range(R // 8):
        for j in range(ncol):
            fp[i * ncol + j] = part[8 * i : 8 * i + 8, 128 * j : 128 * j + 128]

    def wait_tiles(ref, n, sem):
        view = ref.at[pl.ds(0, n)]
        pltpu.make_async_copy(view, view, sem).wait()

    def tile_copy(src, dst, dp, s, r):
        return pltpu.make_async_remote_copy(
            src_ref=src, dst_ref=dst, send_sem=rsem.at[s], recv_sem=rsem.at[r],
            device_id=(dp, t), device_id_type=MESH)

    def slot(to):
        return lax.rem(d - to + 127, 64)

    other_chips(lambda q: tile_copy(fp.at[q], r2.at[slot(2 * q)], 2 * q, 0, 1).start())

    @pl.when(core == 1)
    def _():
        tile_copy(fp.at[chip], r2.at[slot(2 * chip)], 2 * chip, 0, 1).start()

    def rows_of(o):
        return pl.ds(pl.multiple_of(o * tok, tok), tok)

    def ig_copy(n, src, dst, to):
        return pltpu.make_async_remote_copy(
            src_ref=src, dst_ref=dst, send_sem=isem_s.at[n], recv_sem=isem_r.at[n],
            device_id=(d, to), device_id_type=MESH)

    ca, cb = pl.ds(0, half), pl.ds(half, half)
    c_rela = ig_copy(0, igp.at[rows_of(across), ca], rela, left)
    c_relb = ig_copy(1, igp.at[rows_of(across), cb], relb, right)
    c_dira = ig_copy(2, igp.at[rows_of(right), ca], dira, right)
    c_dirb = ig_copy(3, igp.at[rows_of(left), cb], dirb, left)
    for c in (c_rela, c_relb, c_dira, c_dirb):
        c.start()

    @pl.when(core == 0)
    def _():
        r2[63] = fp[chip]
        wait_tiles(r2, 63, rsem.at[1])
        f3[chip] = jnp.sum(r2[...], axis=0)

        def to_chip(q):
            for c in range(2):
                tile_copy(f3.at[chip], f3.at[chip], 2 * q + c, 2, 3).start()

        other_chips(to_chip)
        tile_copy(f3.at[chip], f3.at[chip], 2 * chip + 1, 2, 3).start()

    @pl.when(core == 0)
    def _():
        wait_tiles(f3, 31, rsem.at[3])

    @pl.when(core == 1)
    def _():
        wait_tiles(f3, 32, rsem.at[3])

    ft = jnp.concatenate(
        [jnp.concatenate([f3[i * ncol + j] for j in range(ncol)], axis=1) for i in range(R // 8)], axis=0
    )

    zw = nt * tok
    zr[t, :, 0:zw] = fdot(ft, xsl, NT) * scale
    zr[t, :, zw : zw + R] = lax.dot_general(ft, ft, NT, precision=HIGH, preferred_element_type=F32)
    zcopies = []
    for k in range(1, nt):
        zcopies.append(pltpu.make_async_remote_copy(
            src_ref=zr.at[t], dst_ref=zr.at[t], send_sem=zsem_s.at[k - 1], recv_sem=zsem_r.at[k - 1],
            device_id=(d, lax.rem(t + k, nt)), device_id_type=MESH))
    for c in zcopies:
        c.start()
    for c in zcopies:
        c.wait_recv()
    zt = (zr[0, :, 0:zw] + zr[1, :, 0:zw]) + (zr[2, :, 0:zw] + zr[3, :, 0:zw])
    gs = slice(zw, zw + R)
    gram = (zr[0, :, gs] + zr[1, :, gs]) + (zr[2, :, gs] + zr[3, :, gs])

    cpart = fdot(zt, gv[...], NN)
    ncc = cpart.shape[1] // 128
    nct = R // 8 * ncc
    for i in range(R // 8):
        for j in range(ncc):
            cp[i * ncc + j] = cpart[8 * i : 8 * i + 8, 128 * j : 128 * j + 128]
    other_chips(lambda q: tile_copy(cp.at[q], r4.at[slot(2 * q)], 2 * q, 4, 5).start())

    @pl.when(core == 1)
    def _():
        tile_copy(cp.at[chip], r4.at[slot(2 * chip)], 2 * chip, 4, 5).start()

    @pl.when(core == 0)
    def _():
        r4[63] = cp[chip]

    for e in range(nct - 32):
        to = 8 * e + 1

        @pl.when(d != to)
        def _():
            tile_copy(cp.at[32 + e], r4.at[slot(to)], to, 4, 5).start()

        @pl.when(d == to)
        def _():
            r4[63] = cp[32 + e]

    c_rela.wait_recv()
    suma[...] = (rela[...].astype(F32) + igp[rows_of(left), ca].astype(F32)).astype(BF16)
    c_fina = ig_copy(4, suma, fina, left)
    c_fina.start()
    c_relb.wait_recv()
    sumb[...] = (relb[...].astype(F32) + igp[rows_of(right), cb].astype(F32)).astype(BF16)
    c_finb = ig_copy(5, sumb, finb, right)
    c_finb.start()

    linv = inverse_cholesky(gram)
    bas[...] = lax.dot_general(linv, ft, NN, precision=HIGH, preferred_element_type=F32)

    owner = jnp.logical_or(core == 0, lax.rem(chip, 4) == 0)
    mine = chip * (1 - core) + (32 + lax.div(chip, 4)) * core

    @pl.when(owner)
    def _():
        wait_tiles(r4, 63, rsem.at[5])
        c3[mine] = jnp.sum(r4[...], axis=0)

        def to_chip(q):
            for c in range(2):
                tile_copy(c3.at[mine], c3.at[mine], 2 * q + c, 6, 7).start()

        other_chips(to_chip)
        tile_copy(c3.at[mine], c3.at[mine], 2 * chip + 1 - core, 6, 7).start()

    c_dira.wait_recv()
    c_fina.wait_recv()
    igo[:, ca] = (igp[rows_of(t), ca].astype(F32) + dira[...].astype(F32) + fina[...].astype(F32)).astype(BF16)
    c_dirb.wait_recv()
    c_finb.wait_recv()
    igo[:, cb] = (igp[rows_of(t), cb].astype(F32) + dirb[...].astype(F32) + finb[...].astype(F32)).astype(BF16)

    @pl.when(owner)
    def _():
        wait_tiles(c3, nct - 1, rsem.at[7])

    @pl.when(jnp.logical_not(owner))
    def _():
        wait_tiles(c3, nct, rsem.at[7])

    ct = jnp.concatenate(
        [jnp.concatenate([c3[i * ncc + j] for j in range(ncc)], axis=1) for i in range(R // 8)], axis=0
    )
    cof[...] = lax.dot_general(linv, ct, NN, precision=HIGH, preferred_element_type=F32)

    for c in ycopies + xcopies + zcopies + [c_rela, c_relb, c_dira, c_dirb, c_fina, c_finb]:
        c.wait_send()

    @pl.when(core == 0)
    def _():
        wait_tiles(r2, 31, rsem.at[0])
        wait_tiles(r2, 63, rsem.at[2])

    @pl.when(core == 1)
    def _():
        wait_tiles(r2, 32, rsem.at[0])

    @pl.when(owner)
    def _():
        wait_tiles(r4, nct - 1, rsem.at[4])
        wait_tiles(r4, 63, rsem.at[6])

    @pl.when(jnp.logical_not(owner))
    def _():
        wait_tiles(r4, nct, rsem.at[4])


def write_out(a, b, c, ao, bo, co, sem):
    copies = [pltpu.make_async_copy(s, o, sem.at[i]) for i, (s, o) in enumerate(((a, ao), (b, bo), (c, co)))]
    for copy in copies:
        copy.start()
    for copy in copies:
        copy.wait()


def local(layer_input, pre_grad, weight_in, coeff_prev):
    rows = pre_grad.shape[0]
    scale = 1.0 / math.sqrt(rows * lax.axis_size("dp"))
    tok, width = layer_input.shape
    nt = lax.axis_size("tensor")
    hid = pre_grad.shape[1]
    share = width // nt
    half = width // 2
    nb = 8
    dma = pltpu.SemaphoreType.DMA
    vm = pltpu.VMEM
    any_spec = pl.BlockSpec(memory_space=pl.ANY)
    vmem_spec = pl.BlockSpec(memory_space=pltpu.VMEM)
    ig, basis, coeff = pl.pallas_call(
        functools.partial(kernel, scale),
        out_shape=(
            vm((tok, width), BF16),
            vm((R, share), F32),
            vm((R, hid), F32),
        ),
        in_specs=[any_spec] * 4,
        out_specs=(vmem_spec,) * 3,
        scratch_shapes=[
            vm((tok, width), BF16), vm((rows, hid), BF16), vm((R, hid), F32), vm((width, hid), BF16),
            vm((nt, tok, share), BF16), vm((nt, R, rows), F32),
            vm((32, 8, 128), F32), vm((64, 8, 128), F32), vm((32, 8, 128), F32),
            vm((nt, R, rows + 128), F32),
            vm((40, 8, 128), F32), vm((64, 8, 128), F32), vm((40, 8, 128), F32),
            vm((rows, width), BF16),
            *[vm((tok, half), BF16)] * 8,
            dma((4,)), dma((nb,)),
            dma((3,)), dma((3,)), dma((3,)), dma((3,)), dma((3,)), dma((3,)),
            dma((8,)), dma((6,)), dma((6,)),
        ],
        compiler_params=pltpu.CompilerParams(
            collective_id=0, has_side_effects=True, vmem_limit_bytes=60 * 2**20
        ),
    )(layer_input, pre_grad, weight_in, coeff_prev.T)
    ig, basis, coeff = pl.pallas_call(
        write_out,
        out_shape=tuple(jax.ShapeDtypeStruct(v.shape, v.dtype) for v in (ig, basis, coeff)),
        in_specs=[vmem_spec] * 3,
        out_specs=(any_spec,) * 3,
        scratch_shapes=[dma((3,))],
        compiler_params=pltpu.CompilerParams(vmem_limit_bytes=16 * 2**20),
    )(ig, basis, coeff)
    return ig, basis.T, coeff.T


def solution(mesh):
    return jax.shard_map(
        local,
        mesh=mesh,
        in_specs=(
            P(("dp", "tensor"), None),
            P("dp", "tensor"),
            P(None, "tensor"),
            P("tensor", None),
        ),
        out_specs=(P(("dp", "tensor"), None), P("tensor", None), P("tensor", None)),
        check_vma=False,
    )
```

```python
import functools
import math

import jax
import jax.numpy as jnp
from jax import lax
from jax.experimental import pallas as pl
from jax.experimental.pallas import tpu as pltpu
from jax.sharding import PartitionSpec as P

MESH = pl.DeviceIdType.MESH
HIGH = lax.Precision.HIGHEST
F32 = jnp.float32
BF16 = jnp.bfloat16
NN = (((1,), (0,)), ((), ()))
NT = (((1,), (1,)), ((), ()))
R = 32
NY, NZ = 4, 8


def split3(a):
    hi = a.astype(BF16)
    rest = a - hi.astype(F32)
    mid = rest.astype(BF16)
    low = (rest - mid.astype(F32)).astype(BF16)
    return jnp.concatenate([hi, mid, low], axis=0)


def fdot(a, b, dims):
    r = lax.dot_general(split3(a), b, dims, preferred_element_type=F32)
    return r[0:R] + r[R : 2 * R] + r[2 * R : 3 * R]


def inverse_cholesky(gram):
    n = gram.shape[0]
    row = lax.broadcasted_iota(jnp.int32, (n, n), 0)
    col = lax.broadcasted_iota(jnp.int32, (n, n), 1)
    eye = jnp.where(row == col, 1.0, 0.0).astype(F32)
    m = jnp.concatenate([gram, eye], axis=1)
    below = lax.broadcasted_iota(jnp.int32, (n, 1), 0)
    diag = jnp.zeros((n, 1), F32)
    for j in range(n):
        pivot = m[j : j + 1, j : j + 1]
        column = m[:, j : j + 1]
        diag = jnp.where(below == j, pivot, diag)
        factor = jnp.where(below > j, column / pivot, 0.0)
        m = m - factor * m[j : j + 1, :]
    return m[:, n : 2 * n] / jnp.sqrt(diag)


def far_offset(j, half):
    return half + lax.div(j + 1, 2) * (1 - 2 * lax.rem(j, 2))


def kernel(
    scale,
    x_ref, g_ref, w_ref, q_ref,
    igo, bas, cof,
    xv, gv, qv, wv, xs, yr, fp, r2, f3, zr, cp, r4, c3,
    igp, dira, dirb, rela, relb, suma, sumb, fina, finb,
    lsem, wsem, ysem_s, ysem_r, xsem_s, xsem_r, zsem_s, zsem_r,
    rsem, isem_s, isem_r, far_sem,
):
    d = lax.axis_index("dp")
    t = lax.axis_index("tensor")
    chip = lax.div(d, 2)
    core = lax.rem(d, 2)
    cy, cz = lax.div(chip, NZ), lax.rem(chip, NZ)
    nt = 4
    tok = xv.shape[0]
    share = xs.shape[2]
    half = igp.shape[1] // 2
    left, right, across = lax.rem(t + 3, nt), lax.rem(t + 1, nt), lax.rem(t + 2, nt)

    def other_chips(fn):
        def body(k, carry):
            qy = lax.rem(cy + far_offset(lax.rem(k, NY), NY // 2), NY)
            qz = lax.rem(cz + far_offset(lax.div(k, NY), NZ // 2), NZ)
            fn(qy * NZ + qz)
            return carry

        lax.fori_loop(0, NY * NZ - 1, body, 0)

    bar = pltpu.get_barrier_semaphore()

    def greet(dp, tt):
        pl.semaphore_signal(bar, inc=1, device_id=(dp, tt), device_id_type=MESH)

    def dp_index(dy, dz, dc):
        return (lax.rem(cy + dy, NY) * NZ + lax.rem(cz + dz, NZ)) * 2 + (core + dc - 2 * core * dc)

    z_line = [dp_index(0, dz, 0) for dz in (4, 3, 5, 2, 6, 1, 7)]
    group = [dp_index(dy, 0, dc) for dy in (2, 1, 3, 0) for dc in range(2) if dy or dc]
    for other in z_line + group:
        greet(other, t)
    for k in range(1, nt):
        greet(d, lax.rem(t + k, nt))

    loads = [
        pltpu.make_async_copy(q_ref, qv, lsem.at[0]),
        pltpu.make_async_copy(g_ref, gv, lsem.at[1]),
        pltpu.make_async_copy(x_ref, xv, lsem.at[2]),
        pltpu.make_async_copy(
            x_ref.at[:, pl.ds(pl.multiple_of(t * share, share), share)], xs.at[t], lsem.at[3]
        ),
    ]
    for c in loads:
        c.start()
    nb = wsem.shape[0]
    wb = wv.shape[0] // nb

    def w_copy(b):
        rows = pl.ds(pl.multiple_of(b * wb, wb), wb)
        return pltpu.make_async_copy(w_ref.at[rows], wv.at[rows], wsem.at[b])

    for b in range(nb):
        w_copy(b).start()

    loads[0].wait()
    loads[1].wait()
    yr[t] = fdot(qv[...], gv[...], NT)

    loads[2].wait()

    pl.semaphore_wait(bar, len(z_line) + len(group) + nt - 1)

    ycopies, xcopies = [], []
    for k in range(1, nt):
        to = lax.rem(t + k, nt)
        ycopies.append(pltpu.make_async_remote_copy(
            src_ref=yr.at[t], dst_ref=yr.at[t], send_sem=ysem_s.at[k - 1], recv_sem=ysem_r.at[k - 1],
            device_id=(d, to), device_id_type=MESH))
        xcopies.append(pltpu.make_async_remote_copy(
            src_ref=xv.at[:, pl.ds(pl.multiple_of(to * share, share), share)], dst_ref=xs.at[t],
            send_sem=xsem_s.at[k - 1], recv_sem=xsem_r.at[k - 1],
            device_id=(d, to), device_id_type=MESH))
    for c in ycopies:
        c.start()
    for c in xcopies:
        c.start()

    for other in z_line:
        pl.semaphore_signal(far_sem, inc=1, device_id=(other, t), device_id_type=MESH)

    def ig_block(b, carry):
        w_copy(b).wait()
        rows = pl.ds(pl.multiple_of(b * wb, wb), wb)
        igp[:, rows] = lax.dot_general(gv[...], wv[rows, :], NT, preferred_element_type=F32).astype(BF16)
        return carry

    lax.fori_loop(0, nb, ig_block, 0)

    for c in ycopies:
        c.wait_recv()
    yt = (yr[0] + yr[1]) + (yr[2] + yr[3])
    for c in xcopies:
        c.wait_recv()
    loads[3].wait()

    xsl = xs[...].reshape(nt * tok, share)
    part = fdot(yt, xsl, NN) * scale
    ncol = share // 128
    for i in range(R // 8):
        for j in range(ncol):
            fp[i * ncol + j] = part[8 * i : 8 * i + 8, 128 * j : 128 * j + 128]

    def wait_tiles(ref, n, sem):
        view = ref.at[pl.ds(0, n)]
        pltpu.make_async_copy(view, view, sem).wait()

    def tile_copy(src, dst, dp, s, r):
        return pltpu.make_async_remote_copy(
            src_ref=src, dst_ref=dst, send_sem=rsem.at[s], recv_sem=rsem.at[r],
            device_id=(dp, t), device_id_type=MESH)

    def slot(to):
        return lax.rem(d - to + 127, 64)

    pl.semaphore_wait(far_sem, len(z_line))
    other_chips(lambda q: tile_copy(fp.at[q], r2.at[slot(2 * q)], 2 * q, 0, 1).start())

    @pl.when(core == 1)
    def _():
        tile_copy(fp.at[chip], r2.at[slot(2 * chip)], 2 * chip, 0, 1).start()

    def rows_of(o):
        return pl.ds(pl.multiple_of(o * tok, tok), tok)

    def ig_copy(n, src, dst, to):
        return pltpu.make_async_remote_copy(
            src_ref=src, dst_ref=dst, send_sem=isem_s.at[n], recv_sem=isem_r.at[n],
            device_id=(d, to), device_id_type=MESH)

    ca, cb = pl.ds(0, half), pl.ds(half, half)
    c_rela = ig_copy(0, igp.at[rows_of(across), ca], rela, left)
    c_relb = ig_copy(1, igp.at[rows_of(across), cb], relb, right)
    c_dira = ig_copy(2, igp.at[rows_of(right), ca], dira, right)
    c_dirb = ig_copy(3, igp.at[rows_of(left), cb], dirb, left)
    for c in (c_rela, c_relb, c_dira, c_dirb):
        c.start()

    @pl.when(core == 0)
    def _():
        r2[63] = fp[chip]
        wait_tiles(r2, 63, rsem.at[1])
        f3[chip] = jnp.sum(r2[...], axis=0)

        def to_chip(q):
            for c in range(2):
                tile_copy(f3.at[chip], f3.at[chip], 2 * q + c, 2, 3).start()

        other_chips(to_chip)
        tile_copy(f3.at[chip], f3.at[chip], 2 * chip + 1, 2, 3).start()

    @pl.when(core == 0)
    def _():
        wait_tiles(f3, 31, rsem.at[3])

    @pl.when(core == 1)
    def _():
        wait_tiles(f3, 32, rsem.at[3])

    ft = jnp.concatenate(
        [jnp.concatenate([f3[i * ncol + j] for j in range(ncol)], axis=1) for i in range(R // 8)], axis=0
    )

    zw = nt * tok
    zr[t, :, 0:zw] = fdot(ft, xsl, NT) * scale
    zr[t, :, zw : zw + R] = lax.dot_general(ft, ft, NT, precision=HIGH, preferred_element_type=F32)
    zcopies = []
    for k in range(1, nt):
        zcopies.append(pltpu.make_async_remote_copy(
            src_ref=zr.at[t], dst_ref=zr.at[t], send_sem=zsem_s.at[k - 1], recv_sem=zsem_r.at[k - 1],
            device_id=(d, lax.rem(t + k, nt)), device_id_type=MESH))
    for c in zcopies:
        c.start()
    for c in zcopies:
        c.wait_recv()
    zt = (zr[0, :, 0:zw] + zr[1, :, 0:zw]) + (zr[2, :, 0:zw] + zr[3, :, 0:zw])
    gs = slice(zw, zw + R)
    gram = (zr[0, :, gs] + zr[1, :, gs]) + (zr[2, :, gs] + zr[3, :, gs])

    cpart = fdot(zt, gv[...], NN)
    ncc = cpart.shape[1] // 128
    nct = R // 8 * ncc
    for i in range(R // 8):
        for j in range(ncc):
            cp[i * ncc + j] = cpart[8 * i : 8 * i + 8, 128 * j : 128 * j + 128]
    other_chips(lambda q: tile_copy(cp.at[q], r4.at[slot(2 * q)], 2 * q, 4, 5).start())

    @pl.when(core == 1)
    def _():
        tile_copy(cp.at[chip], r4.at[slot(2 * chip)], 2 * chip, 4, 5).start()

    @pl.when(core == 0)
    def _():
        r4[63] = cp[chip]

    for e in range(nct - 32):
        to = 8 * e + 1

        @pl.when(d != to)
        def _():
            tile_copy(cp.at[32 + e], r4.at[slot(to)], to, 4, 5).start()

        @pl.when(d == to)
        def _():
            r4[63] = cp[32 + e]

    c_rela.wait_recv()
    suma[...] = (rela[...].astype(F32) + igp[rows_of(left), ca].astype(F32)).astype(BF16)
    c_fina = ig_copy(4, suma, fina, left)
    c_fina.start()
    c_relb.wait_recv()
    sumb[...] = (relb[...].astype(F32) + igp[rows_of(right), cb].astype(F32)).astype(BF16)
    c_finb = ig_copy(5, sumb, finb, right)
    c_finb.start()

    linv = inverse_cholesky(gram)
    bas[...] = lax.dot_general(linv, ft, NN, precision=HIGH, preferred_element_type=F32)

    owner = jnp.logical_or(core == 0, lax.rem(chip, 4) == 0)
    mine = chip * (1 - core) + (32 + lax.div(chip, 4)) * core

    @pl.when(owner)
    def _():
        wait_tiles(r4, 63, rsem.at[5])
        c3[mine] = jnp.sum(r4[...], axis=0)

        def to_chip(k, carry):
            q = lax.rem(k, NY) * NZ + lax.div(k, NY)

            @pl.when(q != chip)
            def _():
                for c in (1, 0):
                    tile_copy(c3.at[mine], c3.at[mine], 2 * q + c, 6, 7).start()

            return carry

        lax.fori_loop(0, NY * NZ, to_chip, 0)
        tile_copy(c3.at[mine], c3.at[mine], 2 * chip + 1 - core, 6, 7).start()

    c_dira.wait_recv()
    c_fina.wait_recv()
    igo[:, ca] = (igp[rows_of(t), ca].astype(F32) + dira[...].astype(F32) + fina[...].astype(F32)).astype(BF16)
    c_dirb.wait_recv()
    c_finb.wait_recv()
    igo[:, cb] = (igp[rows_of(t), cb].astype(F32) + dirb[...].astype(F32) + finb[...].astype(F32)).astype(BF16)

    @pl.when(owner)
    def _():
        wait_tiles(c3, nct - 1, rsem.at[7])

    @pl.when(jnp.logical_not(owner))
    def _():
        wait_tiles(c3, nct, rsem.at[7])

    ct = jnp.concatenate(
        [jnp.concatenate([c3[i * ncc + j] for j in range(ncc)], axis=1) for i in range(R // 8)], axis=0
    )
    cof[...] = lax.dot_general(linv, ct, NN, precision=HIGH, preferred_element_type=F32)

    for c in ycopies + xcopies + zcopies + [c_rela, c_relb, c_dira, c_dirb, c_fina, c_finb]:
        c.wait_send()

    @pl.when(core == 0)
    def _():
        wait_tiles(r2, 31, rsem.at[0])
        wait_tiles(r2, 63, rsem.at[2])

    @pl.when(core == 1)
    def _():
        wait_tiles(r2, 32, rsem.at[0])

    @pl.when(owner)
    def _():
        wait_tiles(r4, nct - 1, rsem.at[4])
        wait_tiles(r4, 63, rsem.at[6])

    @pl.when(jnp.logical_not(owner))
    def _():
        wait_tiles(r4, nct, rsem.at[4])


def write_out(a, b, c, ao, bo, co, sem):
    copies = [pltpu.make_async_copy(s, o, sem.at[i]) for i, (s, o) in enumerate(((a, ao), (b, bo), (c, co)))]
    for copy in copies:
        copy.start()
    for copy in copies:
        copy.wait()


def local(layer_input, pre_grad, weight_in, coeff_prev):
    rows = pre_grad.shape[0]
    scale = 1.0 / math.sqrt(rows * lax.axis_size("dp"))
    tok, width = layer_input.shape
    nt = lax.axis_size("tensor")
    hid = pre_grad.shape[1]
    share = width // nt
    half = width // 2
    nb = 8
    dma = pltpu.SemaphoreType.DMA
    vm = pltpu.VMEM
    any_spec = pl.BlockSpec(memory_space=pl.ANY)
    vmem_spec = pl.BlockSpec(memory_space=pltpu.VMEM)
    ig, basis, coeff = pl.pallas_call(
        functools.partial(kernel, scale),
        out_shape=(
            vm((tok, width), BF16),
            vm((R, share), F32),
            vm((R, hid), F32),
        ),
        in_specs=[any_spec] * 4,
        out_specs=(vmem_spec,) * 3,
        scratch_shapes=[
            vm((tok, width), BF16), vm((rows, hid), BF16), vm((R, hid), F32), vm((width, hid), BF16),
            vm((nt, tok, share), BF16), vm((nt, R, rows), F32),
            vm((32, 8, 128), F32), vm((64, 8, 128), F32), vm((32, 8, 128), F32),
            vm((nt, R, rows + 128), F32),
            vm((40, 8, 128), F32), vm((64, 8, 128), F32), vm((40, 8, 128), F32),
            vm((rows, width), BF16),
            *[vm((tok, half), BF16)] * 8,
            dma((4,)), dma((nb,)),
            dma((3,)), dma((3,)), dma((3,)), dma((3,)), dma((3,)), dma((3,)),
            dma((8,)), dma((6,)), dma((6,)), pltpu.SemaphoreType.REGULAR,
        ],
        compiler_params=pltpu.CompilerParams(
            collective_id=0, has_side_effects=True, vmem_limit_bytes=60 * 2**20
        ),
    )(layer_input, pre_grad, weight_in, coeff_prev.T)
    ig, basis, coeff = pl.pallas_call(
        write_out,
        out_shape=tuple(jax.ShapeDtypeStruct(v.shape, v.dtype) for v in (ig, basis, coeff)),
        in_specs=[vmem_spec] * 3,
        out_specs=(any_spec,) * 3,
        scratch_shapes=[dma((3,))],
        compiler_params=pltpu.CompilerParams(vmem_limit_bytes=16 * 2**20),
    )(ig, basis, coeff)
    return ig, basis.T, coeff.T


def solution(mesh):
    return jax.shard_map(
        local,
        mesh=mesh,
        in_specs=(
            P(("dp", "tensor"), None),
            P("dp", "tensor"),
            P(None, "tensor"),
            P("tensor", None),
        ),
        out_specs=(P(("dp", "tensor"), None), P("tensor", None), P("tensor", None)),
        check_vma=False,
    )
```

```python
import functools
import math

import jax
import jax.numpy as jnp
from jax import lax
from jax.experimental import pallas as pl
from jax.experimental.pallas import tpu as pltpu
from jax.sharding import PartitionSpec as P

MESH = pl.DeviceIdType.MESH
HIGH = lax.Precision.HIGHEST
F32 = jnp.float32
BF16 = jnp.bfloat16
NN = (((1,), (0,)), ((), ()))
NT = (((1,), (1,)), ((), ()))
R = 32
NY, NZ = 4, 8


def split3(a):
    hi = a.astype(BF16)
    rest = a - hi.astype(F32)
    mid = rest.astype(BF16)
    low = (rest - mid.astype(F32)).astype(BF16)
    return jnp.concatenate([hi, mid, low], axis=0)


def fdot(a, b, dims):
    r = lax.dot_general(split3(a), b, dims, preferred_element_type=F32)
    return r[0:R] + r[R : 2 * R] + r[2 * R : 3 * R]


def inverse_cholesky(gram):
    n = gram.shape[0]
    row = lax.broadcasted_iota(jnp.int32, (n, n), 0)
    col = lax.broadcasted_iota(jnp.int32, (n, n), 1)
    eye = jnp.where(row == col, 1.0, 0.0).astype(F32)
    m = jnp.concatenate([gram, eye], axis=1)
    below = lax.broadcasted_iota(jnp.int32, (n, 1), 0)
    diag = jnp.zeros((n, 1), F32)
    for j in range(n):
        pivot = m[j : j + 1, j : j + 1]
        column = m[:, j : j + 1]
        diag = jnp.where(below == j, pivot, diag)
        factor = jnp.where(below > j, column / pivot, 0.0)
        m = m - factor * m[j : j + 1, :]
    return m[:, n : 2 * n] / jnp.sqrt(diag)


def kernel(
    scale,
    x_ref, g_ref, w_ref, q_ref,
    igo, bas, cof,
    xv, gv, qv, wv, xs, yr, fp, hp, r2, f3, zr, cp, hc, r4, r5, c3,
    igp, dira, dirb, rela, relb, suma, sumb, fina, finb,
    lsem, wsem, ysem_s, ysem_r, xsem_s, xsem_r, zsem_s, zsem_r,
    rsem, bsem, isem_s, isem_r, far_sem,
):
    d = lax.axis_index("dp")
    t = lax.axis_index("tensor")
    chip = lax.div(d, 2)
    core = lax.rem(d, 2)
    cy, cz = lax.div(chip, NZ), lax.rem(chip, NZ)
    nt = 4
    tok = xv.shape[0]
    share = xs.shape[2]
    half = igp.shape[1] // 2
    left, right, across = lax.rem(t + 3, nt), lax.rem(t + 1, nt), lax.rem(t + 2, nt)

    bar = pltpu.get_barrier_semaphore()

    def greet(dp, tt):
        pl.semaphore_signal(bar, inc=1, device_id=(dp, tt), device_id_type=MESH)

    def dp_index(dy, dz, dc):
        return (lax.rem(cy + dy, NY) * NZ + lax.rem(cz + dz, NZ)) * 2 + (core + dc - 2 * core * dc)

    z_line = [dp_index(0, dz, 0) for dz in (4, 3, 5, 2, 6, 1, 7)]
    group = [dp_index(dy, 0, dc) for dy in (2, 1, 3, 0) for dc in range(2) if dy or dc]
    for other in z_line + group:
        greet(other, t)
    for k in range(1, nt):
        greet(d, lax.rem(t + k, nt))

    loads = [
        pltpu.make_async_copy(q_ref, qv, lsem.at[0]),
        pltpu.make_async_copy(g_ref, gv, lsem.at[1]),
        pltpu.make_async_copy(x_ref, xv, lsem.at[2]),
        pltpu.make_async_copy(
            x_ref.at[:, pl.ds(pl.multiple_of(t * share, share), share)], xs.at[t], lsem.at[3]
        ),
    ]
    for c in loads:
        c.start()
    nb = wsem.shape[0]
    wb = wv.shape[0] // nb

    def w_copy(b):
        rows = pl.ds(pl.multiple_of(b * wb, wb), wb)
        return pltpu.make_async_copy(w_ref.at[rows], wv.at[rows], wsem.at[b])

    for b in range(nb):
        w_copy(b).start()

    loads[0].wait()
    loads[1].wait()
    yr[t] = fdot(qv[...], gv[...], NT)

    loads[2].wait()

    pl.semaphore_wait(bar, len(z_line) + len(group) + nt - 1)

    ycopies, xcopies = [], []
    for k in range(1, nt):
        to = lax.rem(t + k, nt)
        ycopies.append(pltpu.make_async_remote_copy(
            src_ref=yr.at[t], dst_ref=yr.at[t], send_sem=ysem_s.at[k - 1], recv_sem=ysem_r.at[k - 1],
            device_id=(d, to), device_id_type=MESH))
        xcopies.append(pltpu.make_async_remote_copy(
            src_ref=xv.at[:, pl.ds(pl.multiple_of(to * share, share), share)], dst_ref=xs.at[t],
            send_sem=xsem_s.at[k - 1], recv_sem=xsem_r.at[k - 1],
            device_id=(d, to), device_id_type=MESH))
    for c in ycopies:
        c.start()
    for c in xcopies:
        c.start()

    for other in z_line:
        pl.semaphore_signal(far_sem, inc=1, device_id=(other, t), device_id_type=MESH)

    def ig_block(b, carry):
        w_copy(b).wait()
        rows = pl.ds(pl.multiple_of(b * wb, wb), wb)
        igp[:, rows] = lax.dot_general(gv[...], wv[rows, :], NT, preferred_element_type=F32).astype(BF16)
        return carry

    lax.fori_loop(0, nb, ig_block, 0)

    for c in ycopies:
        c.wait_recv()
    yt = (yr[0] + yr[1]) + (yr[2] + yr[3])
    for c in xcopies:
        c.wait_recv()
    loads[3].wait()

    xsl = xs[...].reshape(nt * tok, share)
    part = fdot(yt, xsl, NN) * scale
    ncol = share // 128
    for i in range(R // 8):
        for j in range(ncol):
            fp[i * ncol + j] = part[8 * i : 8 * i + 8, 128 * j : 128 * j + 128]

    def wait_tiles(ref, n, sem):
        view = ref.at[pl.ds(0, n)]
        pltpu.make_async_copy(view, view, sem).wait()

    def tile_copy(src, dst, dp, s, r):
        return pltpu.make_async_remote_copy(
            src_ref=src, dst_ref=dst, send_sem=rsem.at[s], recv_sem=bsem.at[r],
            device_id=(dp, t), device_id_type=MESH)

    oys = [lax.rem(cy + dy, NY) for dy in range(NY)]
    ozs = [lax.rem(cz + dz, NZ) for dz in range(NZ)]
    dev_y = [oy * (2 * NZ) + core for oy in oys]
    dev_z = [2 * oz for oz in ozs]
    tile_y = [lax.rem(oy, 2) * NZ for oy in oys]
    turn_y = [lax.div(oy, 2) for oy in oys]
    turn_z = [lax.rem(oz + NZ // 2, NZ) - oz for oz in ozs]
    more_z = [lax.rem(oz, 4) == 2 for oz in ozs]

    def device(dy, dz):
        return dev_y[dy] + dev_z[dz]

    def tile_of(dy, dz):
        return tile_y[dy] + ozs[dz] + turn_y[dy] * turn_z[dz]

    def more_of(dy, dz):
        return 16 + lax.div(tile_of(dy, dz), 4)

    far_first = [(dy, dz) for dz in (4, 3, 5, 2, 6, 1, 7, 0) for dy in (2, 1, 3, 0) if dy or dz]

    served = [(dy, dz) for dz in (2, 6, 1, 7, 0) for dy in (2, 1, 3, 0)
              if dz in (1, 7) or (dz == 2 and dy != 2) or (dz == 6 and dy == 0) or (dz == 0 and dy)]

    last = NY * NZ - 1
    sibling = 2 * chip + 1 - core
    other_core = 1 - 2 * core
    own_tile = tile_of(0, 0)
    n1, n2 = fp.shape[0] // 2, cp.shape[0] // 2

    swap_f = tile_copy(fp.at[pl.ds((1 - core) * n1, n1)], hp, sibling, 0, 0)
    swap_f.start()
    swap_f.wait_recv()
    half_f = pl.ds(core * n1, n1)
    fp[half_f] = fp[half_f] + hp[...]

    pl.semaphore_wait(far_sem, len(z_line))
    base_f = core * n1
    for dy, dz in far_first:
        tile_copy(fp.at[base_f + tile_of(dy, dz)], r2.at[chip], device(dy, dz), 1, 1).start()
    mine_f = base_f + own_tile
    r2[chip] = fp[mine_f]

    def rows_of(o):
        return pl.ds(pl.multiple_of(o * tok, tok), tok)

    def ig_copy(n, src, dst, to):
        return pltpu.make_async_remote_copy(
            src_ref=src, dst_ref=dst, send_sem=isem_s.at[n], recv_sem=isem_r.at[n],
            device_id=(d, to), device_id_type=MESH)

    ca, cb = pl.ds(0, half), pl.ds(half, half)
    c_rela = ig_copy(0, igp.at[rows_of(across), ca], rela, left)
    c_relb = ig_copy(1, igp.at[rows_of(across), cb], relb, right)
    c_dira = ig_copy(2, igp.at[rows_of(right), ca], dira, right)
    c_dirb = ig_copy(3, igp.at[rows_of(left), cb], dirb, left)
    for c in (c_rela, c_relb, c_dira, c_dirb):
        c.start()

    wait_tiles(r2, last, bsem.at[1])
    f3[mine_f] = jnp.sum(r2[...], axis=0)
    def broadcast(ref, tile, s, r):
        for dy, dz in served:
            for other in (device(dy, dz), device(dy, dz) + other_core):
                tile_copy(ref.at[tile], ref.at[tile], other, s, r).start()
        tile_copy(ref.at[tile], ref.at[tile], sibling, s, r).start()

    broadcast(f3, mine_f, 2, 2)
    wait_tiles(f3, 31, bsem.at[2])

    ft = jnp.concatenate(
        [jnp.concatenate([f3[i * ncol + j] for j in range(ncol)], axis=1) for i in range(R // 8)], axis=0
    )

    zw = nt * tok
    zr[t, :, 0:zw] = fdot(ft, xsl, NT) * scale
    zr[t, :, zw : zw + R] = lax.dot_general(ft, ft, NT, precision=HIGH, preferred_element_type=F32)
    zcopies = []
    for k in range(1, nt):
        zcopies.append(pltpu.make_async_remote_copy(
            src_ref=zr.at[t], dst_ref=zr.at[t], send_sem=zsem_s.at[k - 1], recv_sem=zsem_r.at[k - 1],
            device_id=(d, lax.rem(t + k, nt)), device_id_type=MESH))
    for c in zcopies:
        c.start()
    for c in zcopies:
        c.wait_recv()
    zt = (zr[0, :, 0:zw] + zr[1, :, 0:zw]) + (zr[2, :, 0:zw] + zr[3, :, 0:zw])
    gs = slice(zw, zw + R)
    gram = (zr[0, :, gs] + zr[1, :, gs]) + (zr[2, :, gs] + zr[3, :, gs])

    cpart = fdot(zt, gv[...], NN)
    ncc = cpart.shape[1] // 128
    for i in range(R // 8):
        for j in range(ncc):
            cp[i * ncc + j] = cpart[8 * i : 8 * i + 8, 128 * j : 128 * j + 128]
    swap_c = tile_copy(cp.at[pl.ds((1 - core) * n2, n2)], hc, sibling, 3, 3)
    swap_c.start()
    swap_c.wait_recv()
    half_c = pl.ds(core * n2, n2)
    cp[half_c] = cp[half_c] + hc[...]

    base_c = core * n2
    for dy, dz in far_first:
        tile_copy(cp.at[base_c + tile_of(dy, dz)], r4.at[chip], device(dy, dz), 4, 4).start()
    for z in range(NZ):

        @pl.when(more_z[z])
        def _():
            for dy, dz in far_first:
                if dz == z:
                    tile_copy(cp.at[base_c + more_of(dy, dz)], r5.at[chip], device(dy, dz), 7, 6).start()

    more = more_z[0]
    mine = base_c + own_tile
    mine_more = base_c + more_of(0, 0)
    r4[chip] = cp[mine]

    c_rela.wait_recv()
    suma[...] = (rela[...].astype(F32) + igp[rows_of(left), ca].astype(F32)).astype(BF16)
    c_fina = ig_copy(4, suma, fina, left)
    c_fina.start()
    c_relb.wait_recv()
    sumb[...] = (relb[...].astype(F32) + igp[rows_of(right), cb].astype(F32)).astype(BF16)
    c_finb = ig_copy(5, sumb, finb, right)
    c_finb.start()

    linv = inverse_cholesky(gram)
    bas[...] = lax.dot_general(linv, ft, NN, precision=HIGH, preferred_element_type=F32)

    wait_tiles(r4, last, bsem.at[4])
    c3[mine] = jnp.sum(r4[...], axis=0)
    broadcast(c3, mine, 5, 5)

    @pl.when(more)
    def _():
        r5[chip] = cp[mine_more]
        wait_tiles(r5, last, bsem.at[6])
        c3[mine_more] = jnp.sum(r5[...], axis=0)
        broadcast(c3, mine_more, 6, 5)

    c_dira.wait_recv()
    c_fina.wait_recv()
    igo[:, ca] = (igp[rows_of(t), ca].astype(F32) + dira[...].astype(F32) + fina[...].astype(F32)).astype(BF16)
    c_dirb.wait_recv()
    c_finb.wait_recv()
    igo[:, cb] = (igp[rows_of(t), cb].astype(F32) + dirb[...].astype(F32) + finb[...].astype(F32)).astype(BF16)

    @pl.when(more)
    def _():
        wait_tiles(c3, 2 * n2 - 2, bsem.at[5])

    @pl.when(jnp.logical_not(more))
    def _():
        wait_tiles(c3, 2 * n2 - 1, bsem.at[5])

    ct = jnp.concatenate(
        [jnp.concatenate([c3[i * ncc + j] for j in range(ncc)], axis=1) for i in range(R // 8)], axis=0
    )
    cof[...] = lax.dot_general(linv, ct, NN, precision=HIGH, preferred_element_type=F32)

    for c in ycopies + xcopies + zcopies + [c_rela, c_relb, c_dira, c_dirb, c_fina, c_finb]:
        c.wait_send()
    swap_f.wait_send()
    swap_c.wait_send()
    wait_tiles(f3, 31, rsem.at[1])
    wait_tiles(f3, 31, rsem.at[2])
    wait_tiles(f3, 31, rsem.at[4])
    wait_tiles(f3, 31, rsem.at[5])

    @pl.when(more)
    def _():
        wait_tiles(f3, 31, rsem.at[6])
        wait_tiles(f3, 7, rsem.at[7])

    @pl.when(jnp.logical_not(more))
    def _():
        wait_tiles(f3, 8, rsem.at[7])


def write_out(a, b, c, ao, bo, co, sem):
    copies = [pltpu.make_async_copy(s, o, sem.at[i]) for i, (s, o) in enumerate(((a, ao), (b, bo), (c, co)))]
    for copy in copies:
        copy.start()
    for copy in copies:
        copy.wait()


def local(layer_input, pre_grad, weight_in, coeff_prev):
    rows = pre_grad.shape[0]
    scale = 1.0 / math.sqrt(rows * lax.axis_size("dp"))
    tok, width = layer_input.shape
    nt = lax.axis_size("tensor")
    hid = pre_grad.shape[1]
    share = width // nt
    half = width // 2
    nb = 8
    dma = pltpu.SemaphoreType.DMA
    vm = pltpu.VMEM
    any_spec = pl.BlockSpec(memory_space=pl.ANY)
    vmem_spec = pl.BlockSpec(memory_space=pltpu.VMEM)
    ig, basis, coeff = pl.pallas_call(
        functools.partial(kernel, scale),
        out_shape=(
            vm((tok, width), BF16),
            vm((R, share), F32),
            vm((R, hid), F32),
        ),
        in_specs=[any_spec] * 4,
        out_specs=(vmem_spec,) * 3,
        scratch_shapes=[
            vm((tok, width), BF16), vm((rows, hid), BF16), vm((R, hid), F32), vm((width, hid), BF16),
            vm((nt, tok, share), BF16), vm((nt, R, rows), F32),
            vm((32, 8, 128), F32), vm((16, 8, 128), F32), vm((32, 8, 128), F32), vm((32, 8, 128), F32),
            vm((nt, R, rows + 128), F32),
            vm((40, 8, 128), F32), vm((20, 8, 128), F32), vm((32, 8, 128), F32), vm((32, 8, 128), F32),
            vm((40, 8, 128), F32),
            vm((rows, width), BF16),
            *[vm((tok, half), BF16)] * 8,
            dma((4,)), dma((nb,)),
            dma((3,)), dma((3,)), dma((3,)), dma((3,)), dma((3,)), dma((3,)),
            dma((8,)), dma((7,)), dma((6,)), dma((6,)), pltpu.SemaphoreType.REGULAR,
        ],
        compiler_params=pltpu.CompilerParams(
            collective_id=0, has_side_effects=True, vmem_limit_bytes=60 * 2**20
        ),
    )(layer_input, pre_grad, weight_in, coeff_prev.T)
    ig, basis, coeff = pl.pallas_call(
        write_out,
        out_shape=tuple(jax.ShapeDtypeStruct(v.shape, v.dtype) for v in (ig, basis, coeff)),
        in_specs=[vmem_spec] * 3,
        out_specs=(any_spec,) * 3,
        scratch_shapes=[dma((3,))],
        compiler_params=pltpu.CompilerParams(vmem_limit_bytes=16 * 2**20),
    )(ig, basis, coeff)
    return ig, basis.T, coeff.T


def solution(mesh):
    return jax.shard_map(
        local,
        mesh=mesh,
        in_specs=(
            P(("dp", "tensor"), None),
            P("dp", "tensor"),
            P(None, "tensor"),
            P("tensor", None),
        ),
        out_specs=(P(("dp", "tensor"), None), P("tensor", None), P("tensor", None)),
        check_vma=False,
    )
```

```python
import functools
import math

import jax
import jax.numpy as jnp
from jax import lax
from jax.experimental import pallas as pl
from jax.experimental.pallas import tpu as pltpu
from jax.sharding import PartitionSpec as P

MESH = pl.DeviceIdType.MESH
HIGH = lax.Precision.HIGHEST
F32 = jnp.float32
BF16 = jnp.bfloat16
NN = (((1,), (0,)), ((), ()))
NT = (((1,), (1,)), ((), ()))
R = 32
NY, NZ = 4, 8


def split3(a):
    hi = a.astype(BF16)
    rest = a - hi.astype(F32)
    mid = rest.astype(BF16)
    low = (rest - mid.astype(F32)).astype(BF16)
    return jnp.concatenate([hi, mid, low], axis=0)


def fdot(pieces, b, dims):
    r = lax.dot_general(pieces, b, dims, preferred_element_type=F32)
    return r[0:R] + r[R : 2 * R] + r[2 * R : 3 * R]


def inverse_cholesky(gram):
    n = gram.shape[0]
    row = lax.broadcasted_iota(jnp.int32, (n, n), 0)
    col = lax.broadcasted_iota(jnp.int32, (n, n), 1)
    eye = jnp.where(row == col, 1.0, 0.0).astype(F32)
    m = jnp.concatenate([gram, eye], axis=1)
    below = lax.broadcasted_iota(jnp.int32, (n, 1), 0)
    diag = jnp.zeros((n, 1), F32)
    for j in range(n):
        pivot = m[j : j + 1, j : j + 1]
        column = m[:, j : j + 1]
        diag = jnp.where(below == j, pivot, diag)
        factor = jnp.where(below > j, column / pivot, 0.0)
        m = m - factor * m[j : j + 1, :]
    return m[:, n : 2 * n] / jnp.sqrt(diag)


def kernel(
    scale,
    x_ref, g_ref, w_ref, q_ref,
    igo, bas, cof,
    xv, gv, qv, wv, xs, yp, yr, yf, fp, hp, r2, f3, zr, gr, cp, hc, r4, c3,
    igp, dira, dirb, rela, relb, suma, sumb, fina, finb,
    lsem, wsem, ysem_s, ysem_r, xsem_s, xsem_r, zsem_s, zsem_r, gsem_s, gsem_r, fsem_s, fsem_r,
    rsem, bsem, isem_s, isem_r, far_sem,
):
    d = lax.axis_index("dp")
    t = lax.axis_index("tensor")
    chip = lax.div(d, 2)
    core = lax.rem(d, 2)
    cy, cz = lax.div(chip, NZ), lax.rem(chip, NZ)
    nt = 4
    tok = xv.shape[0]
    share = xs.shape[2]
    half = igp.shape[1] // 2
    left, right, across = lax.rem(t + 3, nt), lax.rem(t + 1, nt), lax.rem(t + 2, nt)

    bar = pltpu.get_barrier_semaphore()

    def greet(dp, tt):
        pl.semaphore_signal(bar, inc=1, device_id=(dp, tt), device_id_type=MESH)

    def dp_index(dy, dz, dc):
        return (lax.rem(cy + dy, NY) * NZ + lax.rem(cz + dz, NZ)) * 2 + (core + dc - 2 * core * dc)

    z_line = [dp_index(0, dz, 0) for dz in (4, 3, 5, 2, 6, 1, 7)]
    group = [dp_index(dy, 0, dc) for dy in (2, 1, 3, 0) for dc in range(2) if dy or dc]
    for k in range(1, nt):
        greet(d, lax.rem(t + k, nt))
    for other in z_line + group:
        greet(other, t)

    loads = [
        pltpu.make_async_copy(q_ref, qv, lsem.at[0]),
        pltpu.make_async_copy(g_ref, gv, lsem.at[1]),
        pltpu.make_async_copy(x_ref, xv, lsem.at[2]),
        pltpu.make_async_copy(
            x_ref.at[:, pl.ds(pl.multiple_of(t * share, share), share)], xs.at[t], lsem.at[3]
        ),
    ]
    for c in loads:
        c.start()
    nb = wsem.shape[0]
    wb = wv.shape[0] // nb

    def w_copy(b):
        rows = pl.ds(pl.multiple_of(b * wb, wb), wb)
        return pltpu.make_async_copy(w_ref.at[rows], wv.at[rows], wsem.at[b])

    for b in range(nb):
        w_copy(b).start()

    loads[0].wait()
    loads[1].wait()
    yp[...] = fdot(split3(qv[...]), gv[...], NT)
    ranks = R // nt

    def ranks_of(o):
        return pl.ds(pl.multiple_of(o * ranks, ranks), ranks)

    yr[t] = yp[ranks_of(t)]

    loads[2].wait()

    pl.semaphore_wait(bar, len(z_line) + len(group) + nt - 1)

    ycopies, xcopies = [], []
    for k in range(1, nt):
        to = lax.rem(t + k, nt)
        ycopies.append(pltpu.make_async_remote_copy(
            src_ref=yp.at[ranks_of(to)], dst_ref=yr.at[t], send_sem=ysem_s.at[k - 1], recv_sem=ysem_r.at[k - 1],
            device_id=(d, to), device_id_type=MESH))
        xcopies.append(pltpu.make_async_remote_copy(
            src_ref=xv.at[:, pl.ds(pl.multiple_of(to * share, share), share)], dst_ref=xs.at[t],
            send_sem=xsem_s.at[k - 1], recv_sem=xsem_r.at[k - 1],
            device_id=(d, to), device_id_type=MESH))
    for c in ycopies:
        c.start()
    for c in xcopies:
        c.start()

    for other in z_line:
        pl.semaphore_signal(far_sem, inc=1, device_id=(other, t), device_id_type=MESH)

    def ig_block(b, carry):
        w_copy(b).wait()
        rows = pl.ds(pl.multiple_of(b * wb, wb), wb)
        igp[:, rows] = lax.dot_general(gv[...], wv[rows, :], NT, preferred_element_type=F32).astype(BF16)
        return carry

    lax.fori_loop(0, nb // 2, ig_block, 0)
    for c in ycopies:
        c.wait_recv()
    yf[t] = (yr[0] + yr[1]) + (yr[2] + yr[3])
    fcopies = []
    for k in range(1, nt):
        fcopies.append(pltpu.make_async_remote_copy(
            src_ref=yf.at[t], dst_ref=yf.at[t], send_sem=fsem_s.at[k - 1], recv_sem=fsem_r.at[k - 1],
            device_id=(d, lax.rem(t + k, nt)), device_id_type=MESH))
    for c in fcopies:
        c.start()
    lax.fori_loop(nb // 2, nb, ig_block, 0)

    for c in fcopies:
        c.wait_recv()
    yt = yf[...].reshape(R, nt * tok)
    for c in xcopies:
        c.wait_recv()
    loads[3].wait()

    def wait_tiles(ref, n, sem):
        view = ref.at[pl.ds(0, n)]
        pltpu.make_async_copy(view, view, sem).wait()

    def tile_copy(src, dst, dp, s, r):
        return pltpu.make_async_remote_copy(
            src_ref=src, dst_ref=dst, send_sem=rsem.at[s], recv_sem=bsem.at[r],
            device_id=(dp, t), device_id_type=MESH)

    oys = [lax.rem(cy + dy, NY) for dy in range(NY)]
    ozs = [lax.rem(cz + dz, NZ) for dz in range(NZ)]
    dev_y = [oy * (2 * NZ) + core for oy in oys]
    dev_z = [2 * oz for oz in ozs]
    tile_y = [lax.rem(oy, 2) * NZ for oy in oys]
    turn_y = [lax.div(oy, 2) for oy in oys]
    turn_z = [lax.rem(oz + NZ // 2, NZ) - oz for oz in ozs]

    def device(dy, dz):
        return dev_y[dy] + dev_z[dz]

    def tile_of(dy, dz):
        return tile_y[dy] + ozs[dz] + turn_y[dy] * turn_z[dz]

    far_first = [(dy, dz) for dz in (4, 3, 5, 2, 6, 1, 7, 0) for dy in (2, 1, 3, 0) if dy or dz]

    served = [(dy, dz) for dz in (2, 6, 1, 7, 0) for dy in (2, 1, 3, 0)
              if dz in (1, 7) or (dz == 2 and dy != 2) or (dz == 6 and dy == 0) or (dz == 0 and dy)]

    last = NY * NZ - 1
    pieces = fp.shape[0] // 2
    ys = split3(yt)
    width_f = share // 2
    sibling = 2 * chip + 1 - core
    other_core = 1 - 2 * core
    own_tile = tile_of(0, 0)

    def factor_half(h):
        columns = pl.ds(pl.multiple_of(h * width_f, width_f), width_f)
        part = fdot(ys, xs[:, :, columns].reshape(nt * tok, width_f), NN) * scale
        for k in range(pieces):
            i, j = k % 4, k // 4
            fp[h * pieces + k] = part[8 * i : 8 * i + 8, 128 * j : 128 * j + 128]

    def half_of(h):
        return pl.ds(h * pieces, pieces)

    factor_half(1 - core)
    swap_f = tile_copy(fp.at[half_of(1 - core)], hp, sibling, 0, 0)
    swap_f.start()
    factor_half(core)
    swap_f.wait_recv()
    fp[half_of(core)] = fp[half_of(core)] + hp[...]

    pl.semaphore_wait(far_sem, len(z_line))
    base = core * pieces
    for dy, dz in far_first:
        tile_copy(fp.at[base + tile_of(dy, dz)], r2.at[chip], device(dy, dz), 1, 1).start()
    mine = base + own_tile
    r2[chip] = fp[mine]

    def rows_of(o):
        return pl.ds(pl.multiple_of(o * tok, tok), tok)

    def ig_copy(n, src, dst, to):
        return pltpu.make_async_remote_copy(
            src_ref=src, dst_ref=dst, send_sem=isem_s.at[n], recv_sem=isem_r.at[n],
            device_id=(d, to), device_id_type=MESH)

    ca, cb = pl.ds(0, half), pl.ds(half, half)
    c_rela = ig_copy(0, igp.at[rows_of(across), ca], rela, left)
    c_relb = ig_copy(1, igp.at[rows_of(across), cb], relb, right)
    c_dira = ig_copy(2, igp.at[rows_of(right), ca], dira, right)
    c_dirb = ig_copy(3, igp.at[rows_of(left), cb], dirb, left)
    for c in (c_rela, c_relb, c_dira, c_dirb):
        c.start()

    wait_tiles(r2, last, bsem.at[1])
    f3[mine] = jnp.sum(r2[...], axis=0)
    def broadcast(ref, tile, s, r):
        for dy, dz in served:
            for other in (device(dy, dz), device(dy, dz) + other_core):
                tile_copy(ref.at[tile], ref.at[tile], other, s, r).start()
        tile_copy(ref.at[tile], ref.at[tile], sibling, s, r).start()

    broadcast(f3, mine, 2, 2)
    wait_tiles(f3, 31, bsem.at[2])

    ft = jnp.concatenate(
        [jnp.concatenate([f3[4 * j + i] for j in range(share // 128)], axis=1) for i in range(4)], axis=0
    )
    xsl = xs[...].reshape(nt * tok, share)

    zr[t] = fdot(split3(ft), xsl, NT) * scale
    zcopies, gcopies = [], []
    for k in range(1, nt):
        zcopies.append(pltpu.make_async_remote_copy(
            src_ref=zr.at[t], dst_ref=zr.at[t], send_sem=zsem_s.at[k - 1], recv_sem=zsem_r.at[k - 1],
            device_id=(d, lax.rem(t + k, nt)), device_id_type=MESH))
    for c in zcopies:
        c.start()
    gr[t, :, 0:R] = lax.dot_general(ft, ft, NT, precision=HIGH, preferred_element_type=F32)
    for k in range(1, nt):
        gcopies.append(pltpu.make_async_remote_copy(
            src_ref=gr.at[t], dst_ref=gr.at[t], send_sem=gsem_s.at[k - 1], recv_sem=gsem_r.at[k - 1],
            device_id=(d, lax.rem(t + k, nt)), device_id_type=MESH))
    for c in gcopies:
        c.start()
    for c in zcopies:
        c.wait_recv()
    zt = (zr[0] + zr[1]) + (zr[2] + zr[3])

    zs = split3(zt)
    width_c = gv.shape[1] // 2
    edge_c = width_c - 128

    def coeff_half(h):
        columns = pl.ds(pl.multiple_of(h * width_c, 128), width_c)
        part = fdot(zs, gv[:, columns], NN)
        for k in range(pieces):
            i, j = k % 4, k // 4
            cp[h * pieces + k, 0:8] = part[8 * i : 8 * i + 8, 128 * j : 128 * j + 128]
            cp[h * pieces + k, 8:10] = part[2 * k : 2 * k + 2, edge_c:width_c]

    coeff_half(1 - core)
    swap_c = tile_copy(cp.at[half_of(1 - core)], hc, sibling, 3, 3)
    swap_c.start()
    coeff_half(core)
    swap_c.wait_recv()
    cp[half_of(core)] = cp[half_of(core)] + hc[...]
    for dy, dz in far_first:
        tile_copy(cp.at[base + tile_of(dy, dz)], r4.at[chip], device(dy, dz), 4, 4).start()
    r4[chip] = cp[mine]

    c_rela.wait_recv()
    suma[...] = (rela[...].astype(F32) + igp[rows_of(left), ca].astype(F32)).astype(BF16)
    c_fina = ig_copy(4, suma, fina, left)
    c_fina.start()
    c_relb.wait_recv()
    sumb[...] = (relb[...].astype(F32) + igp[rows_of(right), cb].astype(F32)).astype(BF16)
    c_finb = ig_copy(5, sumb, finb, right)
    c_finb.start()

    for c in gcopies:
        c.wait_recv()
    gs = slice(0, R)
    gram = (gr[0, :, gs] + gr[1, :, gs]) + (gr[2, :, gs] + gr[3, :, gs])
    linv = inverse_cholesky(gram)
    bas[...] = lax.dot_general(linv, ft, NN, precision=HIGH, preferred_element_type=F32)

    wait_tiles(r4, last, bsem.at[4])
    c3[mine] = jnp.sum(r4[...], axis=0)
    broadcast(c3, mine, 5, 5)

    c_dira.wait_recv()
    c_fina.wait_recv()
    igo[:, ca] = (igp[rows_of(t), ca].astype(F32) + dira[...].astype(F32) + fina[...].astype(F32)).astype(BF16)
    c_dirb.wait_recv()
    c_finb.wait_recv()
    igo[:, cb] = (igp[rows_of(t), cb].astype(F32) + dirb[...].astype(F32) + finb[...].astype(F32)).astype(BF16)

    wait_tiles(c3, 31, bsem.at[5])
    blocks = []
    for h in range(2):
        for j in range(4):
            blocks.append(jnp.concatenate([c3[h * pieces + 4 * j + i, 0:8] for i in range(4)], axis=0))
        blocks.append(jnp.concatenate([c3[h * pieces + k, 8:10] for k in range(pieces)], axis=0))
    ct = jnp.concatenate(blocks, axis=1)
    cof[...] = lax.dot_general(linv, ct, NN, precision=HIGH, preferred_element_type=F32)

    for c in ycopies + fcopies + xcopies + zcopies + gcopies + [c_rela, c_relb, c_dira, c_dirb, c_fina, c_finb]:
        c.wait_send()
    swap_f.wait_send()
    swap_c.wait_send()
    wait_tiles(f3, 31, rsem.at[1])
    wait_tiles(f3, 31, rsem.at[2])
    wait_tiles(c3, 31, rsem.at[4])
    wait_tiles(c3, 31, rsem.at[5])


def write_out(a, b, c, ao, bo, co, sem):
    copies = [pltpu.make_async_copy(s, o, sem.at[i]) for i, (s, o) in enumerate(((a, ao), (b, bo), (c, co)))]
    for copy in copies:
        copy.start()
    for copy in copies:
        copy.wait()


def local(layer_input, pre_grad, weight_in, coeff_prev):
    rows = pre_grad.shape[0]
    scale = 1.0 / math.sqrt(rows * lax.axis_size("dp"))
    tok, width = layer_input.shape
    nt = lax.axis_size("tensor")
    hid = pre_grad.shape[1]
    share = width // nt
    half = width // 2
    nb = 8
    dma = pltpu.SemaphoreType.DMA
    vm = pltpu.VMEM
    any_spec = pl.BlockSpec(memory_space=pl.ANY)
    vmem_spec = pl.BlockSpec(memory_space=pltpu.VMEM)
    ig, basis, coeff = pl.pallas_call(
        functools.partial(kernel, scale),
        out_shape=(
            vm((tok, width), BF16),
            vm((R, share), F32),
            vm((R, hid), F32),
        ),
        in_specs=[any_spec] * 4,
        out_specs=(vmem_spec,) * 3,
        scratch_shapes=[
            vm((tok, width), BF16), vm((rows, hid), BF16), vm((R, hid), F32), vm((width, hid), BF16),
            vm((nt, tok, share), BF16), vm((R, rows), F32), *[vm((nt, R // nt, rows), F32)] * 2,
            vm((32, 8, 128), F32), vm((16, 8, 128), F32), vm((32, 8, 128), F32), vm((32, 8, 128), F32),
            vm((nt, R, rows), F32), vm((nt, R, 128), F32),
            vm((32, 10, 128), F32), vm((16, 10, 128), F32), vm((32, 10, 128), F32), vm((32, 10, 128), F32),
            vm((rows, width), BF16),
            *[vm((tok, half), BF16)] * 8,
            dma((4,)), dma((nb,)),
            *[dma((3,))] * 10,
            dma((6,)), dma((6,)), dma((6,)), dma((6,)), pltpu.SemaphoreType.REGULAR,
        ],
        compiler_params=pltpu.CompilerParams(
            collective_id=0, has_side_effects=True, vmem_limit_bytes=60 * 2**20
        ),
    )(layer_input, pre_grad, weight_in, coeff_prev.T)
    ig, basis, coeff = pl.pallas_call(
        write_out,
        out_shape=tuple(jax.ShapeDtypeStruct(v.shape, v.dtype) for v in (ig, basis, coeff)),
        in_specs=[vmem_spec] * 3,
        out_specs=(any_spec,) * 3,
        scratch_shapes=[dma((3,))],
        compiler_params=pltpu.CompilerParams(vmem_limit_bytes=16 * 2**20),
    )(ig, basis, coeff)
    return ig, basis.T, coeff.T


def solution(mesh):
    return jax.shard_map(
        local,
        mesh=mesh,
        in_specs=(
            P(("dp", "tensor"), None),
            P("dp", "tensor"),
            P(None, "tensor"),
            P("tensor", None),
        ),
        out_specs=(P(("dp", "tensor"), None), P("tensor", None), P("tensor", None)),
        check_vma=False,
    )
```

```python
import functools
import math

import jax
import jax.numpy as jnp
from jax import lax
from jax.experimental import pallas as pl
from jax.experimental.pallas import tpu as pltpu
from jax.sharding import PartitionSpec as P

MESH = pl.DeviceIdType.MESH
HIGH = lax.Precision.HIGHEST
F32 = jnp.float32
BF16 = jnp.bfloat16
NN = (((1,), (0,)), ((), ()))
NT = (((1,), (1,)), ((), ()))
R = 32
NY, NZ = 4, 8


def split3(a):
    hi = a.astype(BF16)
    rest = a - hi.astype(F32)
    mid = rest.astype(BF16)
    low = (rest - mid.astype(F32)).astype(BF16)
    return jnp.concatenate([hi, mid, low], axis=0)


def fdot(pieces, b, dims):
    r = lax.dot_general(pieces, b, dims, preferred_element_type=F32)
    return r[0:R] + r[R : 2 * R] + r[2 * R : 3 * R]


def inverse_cholesky(gram):
    n = gram.shape[0]
    row = lax.broadcasted_iota(jnp.int32, (n, n), 0)
    col = lax.broadcasted_iota(jnp.int32, (n, n), 1)
    eye = jnp.where(row == col, 1.0, 0.0).astype(F32)
    m = jnp.concatenate([gram, eye], axis=1)
    below = lax.broadcasted_iota(jnp.int32, (n, 1), 0)
    diag = jnp.zeros((n, 1), F32)
    for j in range(n):
        pivot = m[j : j + 1, j : j + 1]
        column = m[:, j : j + 1]
        diag = jnp.where(below == j, pivot, diag)
        factor = jnp.where(below > j, column / pivot, 0.0)
        m = m - factor * m[j : j + 1, :]
    return m[:, n : 2 * n] / jnp.sqrt(diag)


def kernel(
    scale,
    x_ref, g_ref, w_ref, q_ref,
    igo, bas, cof,
    xv, gv, qv, wv, xh, xz, yp, yr, yf, fp, r2, f3, zr, gr, cp, hc, r4, c3,
    igp, dira, dirb, rela, relb, suma, sumb, fina, finb,
    lsem, wsem, ysem_s, ysem_r, xsem_s, xsem_r, zsem_s, zsem_r, gsem_s, gsem_r, fsem_s, fsem_r,
    rsem, bsem, isem_s, isem_r, far_sem,
):
    d = lax.axis_index("dp")
    t = lax.axis_index("tensor")
    chip = lax.div(d, 2)
    core = lax.rem(d, 2)
    cy, cz = lax.div(chip, NZ), lax.rem(chip, NZ)
    nt = 4
    tok = xv.shape[0]
    hw = xz.shape[3]
    share = 2 * hw
    half = igp.shape[1] // 2
    left, right, across = lax.rem(t + 3, nt), lax.rem(t + 1, nt), lax.rem(t + 2, nt)

    bar = pltpu.get_barrier_semaphore()

    def greet(dp, tt):
        pl.semaphore_signal(bar, inc=1, device_id=(dp, tt), device_id_type=MESH)

    def dp_index(dy, dz, dc):
        return (lax.rem(cy + dy, NY) * NZ + lax.rem(cz + dz, NZ)) * 2 + (core + dc - 2 * core * dc)

    z_line = [dp_index(0, dz, 0) for dz in (4, 3, 5, 2, 6, 1, 7)]
    group = [dp_index(dy, 0, dc) for dy in (2, 1, 3, 0) for dc in range(2) if dy or dc]
    sibling = 2 * chip + 1 - core
    for k in range(1, nt):
        greet(d, lax.rem(t + k, nt))
        greet(sibling, lax.rem(t + k, nt))
    for other in z_line + group:
        greet(other, t)

    loads = [
        pltpu.make_async_copy(q_ref, qv, lsem.at[0]),
        pltpu.make_async_copy(g_ref, gv, lsem.at[1]),
        pltpu.make_async_copy(x_ref, xv, lsem.at[2]),
        pltpu.make_async_copy(
            x_ref.at[:, pl.ds(pl.multiple_of(t * share + core * hw, hw), hw)], xh.at[core, t], lsem.at[3]
        ),
    ]
    for c in loads:
        c.start()
    nb = wsem.shape[0]
    wb = wv.shape[0] // nb

    def w_copy(b):
        rows = pl.ds(pl.multiple_of(b * wb, wb), wb)
        return pltpu.make_async_copy(w_ref.at[rows], wv.at[rows], wsem.at[b])

    for b in range(nb):
        w_copy(b).start()

    loads[0].wait()
    loads[1].wait()
    yp[...] = fdot(split3(qv[...]), gv[...], NT)
    ranks = R // nt

    def ranks_of(o):
        return pl.ds(pl.multiple_of(o * ranks, ranks), ranks)

    yr[t] = yp[ranks_of(t)]

    loads[2].wait()

    pl.semaphore_wait(bar, len(z_line) + len(group) + 2 * (nt - 1))

    def x_copy(to, dc, n):
        half = core + dc - 2 * core * dc
        return pltpu.make_async_remote_copy(
            src_ref=xv.at[:, pl.ds(pl.multiple_of(to * share + half * hw, hw), hw)], dst_ref=xh.at[core, t],
            send_sem=xsem_s.at[n], recv_sem=xsem_r.at[n],
            device_id=(d if dc == 0 else sibling, to), device_id_type=MESH)

    ycopies, xcopies = [], []
    for k in range(1, nt):
        to = lax.rem(t + k, nt)
        ycopies.append(pltpu.make_async_remote_copy(
            src_ref=yp.at[ranks_of(to)], dst_ref=yr.at[t], send_sem=ysem_s.at[k - 1], recv_sem=ysem_r.at[k - 1],
            device_id=(d, to), device_id_type=MESH))
        for dc in range(2):
            xcopies.append(x_copy(to, dc, 2 * k - 2 + dc))
    xcopies.append(x_copy(t, 1, 6))
    for c in ycopies:
        c.start()
    for c in xcopies:
        c.start()

    for other in z_line:
        pl.semaphore_signal(far_sem, inc=1, device_id=(other, t), device_id_type=MESH)

    def ig_block(b, carry):
        w_copy(b).wait()
        rows = pl.ds(pl.multiple_of(b * wb, wb), wb)
        igp[:, rows] = lax.dot_general(gv[...], wv[rows, :], NT, preferred_element_type=F32).astype(BF16)
        return carry

    lax.fori_loop(0, nb // 2, ig_block, 0)
    for c in ycopies:
        c.wait_recv()
    yf[core, t] = (yr[0] + yr[1]) + (yr[2] + yr[3])
    fcopies = []
    for k in range(nt):
        for dc in range(2):
            if k or dc:
                fcopies.append(pltpu.make_async_remote_copy(
                    src_ref=yf.at[core, t], dst_ref=yf.at[core, t],
                    send_sem=fsem_s.at[2 * k + dc - 1], recv_sem=fsem_r.at[2 * k + dc - 1],
                    device_id=(d if dc == 0 else sibling, lax.rem(t + k, nt)), device_id_type=MESH))
    for c in fcopies:
        c.start()
    lax.fori_loop(nb // 2, nb, ig_block, 0)

    for c in fcopies:
        c.wait_recv()
    yt = jnp.concatenate([yf[g].reshape(R, nt * tok) for g in range(2)], axis=1)
    for c in xcopies:
        c.wait_recv()
    loads[3].wait()

    def wait_tiles(ref, n, sem):
        view = ref.at[pl.ds(0, n)]
        pltpu.make_async_copy(view, view, sem).wait()

    def tile_copy(src, dst, dp, s, r):
        return pltpu.make_async_remote_copy(
            src_ref=src, dst_ref=dst, send_sem=rsem.at[s], recv_sem=bsem.at[r],
            device_id=(dp, t), device_id_type=MESH)

    oys = [lax.rem(cy + dy, NY) for dy in range(NY)]
    ozs = [lax.rem(cz + dz, NZ) for dz in range(NZ)]
    dev_y = [oy * (2 * NZ) + core for oy in oys]
    dev_z = [2 * oz for oz in ozs]
    tile_y = [lax.rem(oy, 2) * NZ for oy in oys]
    turn_y = [lax.div(oy, 2) for oy in oys]
    turn_z = [lax.rem(oz + NZ // 2, NZ) - oz for oz in ozs]

    def device(dy, dz):
        return dev_y[dy] + dev_z[dz]

    def tile_of(dy, dz):
        return tile_y[dy] + ozs[dz] + turn_y[dy] * turn_z[dz]

    far_first = [(dy, dz) for dz in (4, 3, 5, 2, 6, 1, 7, 0) for dy in (2, 1, 3, 0) if dy or dz]

    served = [(dy, dz) for dz in (2, 6, 1, 7, 0) for dy in (2, 1, 3, 0)
              if dz in (1, 7) or (dz == 2 and dy != 2) or (dz == 6 and dy == 0) or (dz == 0 and dy)]

    last = NY * NZ - 1
    pieces = fp.shape[0]
    other_core = 1 - 2 * core
    own_tile = tile_of(0, 0)

    part = fdot(split3(yt), xh[...].reshape(2 * nt * tok, hw), NN) * scale
    for k in range(pieces):
        i, j = k % 4, k // 4
        fp[k] = part[8 * i : 8 * i + 8, 128 * j : 128 * j + 128]

    def half_of(h):
        return pl.ds(h * pieces, pieces)

    pl.semaphore_wait(far_sem, len(z_line))
    base = core * pieces
    for dy, dz in far_first:
        tile_copy(fp.at[tile_of(dy, dz)], r2.at[chip], device(dy, dz), 1, 1).start()
    mine = base + own_tile
    r2[chip] = fp[own_tile]

    x_swap = pltpu.make_async_remote_copy(
        src_ref=xh.at[1 - core], dst_ref=xz.at[core], send_sem=xsem_s.at[7], recv_sem=xsem_r.at[7],
        device_id=(sibling, t), device_id_type=MESH)
    x_swap.start()
    x_keep = pltpu.make_async_copy(xh.at[core], xz.at[core], lsem.at[4])
    x_keep.start()

    def rows_of(o):
        return pl.ds(pl.multiple_of(o * tok, tok), tok)

    def ig_copy(n, src, dst, to):
        return pltpu.make_async_remote_copy(
            src_ref=src, dst_ref=dst, send_sem=isem_s.at[n], recv_sem=isem_r.at[n],
            device_id=(d, to), device_id_type=MESH)

    ca, cb = pl.ds(0, half), pl.ds(half, half)
    c_rela = ig_copy(0, igp.at[rows_of(across), ca], rela, left)
    c_relb = ig_copy(1, igp.at[rows_of(across), cb], relb, right)
    c_dira = ig_copy(2, igp.at[rows_of(right), ca], dira, right)
    c_dirb = ig_copy(3, igp.at[rows_of(left), cb], dirb, left)
    for c in (c_rela, c_relb, c_dira, c_dirb):
        c.start()

    wait_tiles(r2, last, bsem.at[1])
    f3[mine] = jnp.sum(r2[...], axis=0)
    def broadcast(ref, tile, s, r):
        for dy, dz in served:
            for other in (device(dy, dz), device(dy, dz) + other_core):
                tile_copy(ref.at[tile], ref.at[tile], other, s, r).start()
        tile_copy(ref.at[tile], ref.at[tile], sibling, s, r).start()

    broadcast(f3, mine, 2, 2)
    wait_tiles(f3, 31, bsem.at[2])

    def columns(h):
        return jnp.concatenate(
            [jnp.concatenate([f3[h * pieces + 4 * j + i] for j in range(hw // 128)], axis=1) for i in range(4)], axis=0
        )

    x_keep.wait()
    x_swap.wait_recv()
    halves = [columns(0), columns(1)]
    ft = jnp.concatenate(halves, axis=1)
    z_parts = [fdot(split3(halves[h]), xz[h].reshape(nt * tok, hw), NT) for h in range(2)]

    zr[t] = (z_parts[0] + z_parts[1]) * scale
    zcopies, gcopies = [], []
    for k in range(1, nt):
        zcopies.append(pltpu.make_async_remote_copy(
            src_ref=zr.at[t], dst_ref=zr.at[t], send_sem=zsem_s.at[k - 1], recv_sem=zsem_r.at[k - 1],
            device_id=(d, lax.rem(t + k, nt)), device_id_type=MESH))
    for c in zcopies:
        c.start()
    gr[t, :, 0:R] = lax.dot_general(ft, ft, NT, precision=HIGH, preferred_element_type=F32)
    for k in range(1, nt):
        gcopies.append(pltpu.make_async_remote_copy(
            src_ref=gr.at[t], dst_ref=gr.at[t], send_sem=gsem_s.at[k - 1], recv_sem=gsem_r.at[k - 1],
            device_id=(d, lax.rem(t + k, nt)), device_id_type=MESH))
    for c in gcopies:
        c.start()
    for c in zcopies:
        c.wait_recv()
    zt = (zr[0] + zr[1]) + (zr[2] + zr[3])

    zs = split3(zt)
    width_c = gv.shape[1] // 2
    edge_c = width_c - 128

    def coeff_half(h):
        columns = pl.ds(pl.multiple_of(h * width_c, 128), width_c)
        part = fdot(zs, gv[:, columns], NN)
        for k in range(pieces):
            i, j = k % 4, k // 4
            cp[h * pieces + k, 0:8] = part[8 * i : 8 * i + 8, 128 * j : 128 * j + 128]
            cp[h * pieces + k, 8:10] = part[2 * k : 2 * k + 2, edge_c:width_c]

    coeff_half(1 - core)
    swap_c = tile_copy(cp.at[half_of(1 - core)], hc, sibling, 3, 3)
    swap_c.start()
    coeff_half(core)
    swap_c.wait_recv()
    cp[half_of(core)] = cp[half_of(core)] + hc[...]
    for dy, dz in far_first:
        tile_copy(cp.at[base + tile_of(dy, dz)], r4.at[chip], device(dy, dz), 4, 4).start()
    r4[chip] = cp[mine]

    c_rela.wait_recv()
    suma[...] = (rela[...].astype(F32) + igp[rows_of(left), ca].astype(F32)).astype(BF16)
    c_fina = ig_copy(4, suma, fina, left)
    c_fina.start()
    c_relb.wait_recv()
    sumb[...] = (relb[...].astype(F32) + igp[rows_of(right), cb].astype(F32)).astype(BF16)
    c_finb = ig_copy(5, sumb, finb, right)
    c_finb.start()

    for c in gcopies:
        c.wait_recv()
    gs = slice(0, R)
    gram = (gr[0, :, gs] + gr[1, :, gs]) + (gr[2, :, gs] + gr[3, :, gs])
    linv = inverse_cholesky(gram)
    bas[...] = lax.dot_general(linv, ft, NN, precision=HIGH, preferred_element_type=F32)

    wait_tiles(r4, last, bsem.at[4])
    c3[mine] = jnp.sum(r4[...], axis=0)
    broadcast(c3, mine, 5, 5)

    c_dira.wait_recv()
    c_fina.wait_recv()
    igo[:, ca] = (igp[rows_of(t), ca].astype(F32) + dira[...].astype(F32) + fina[...].astype(F32)).astype(BF16)
    c_dirb.wait_recv()
    c_finb.wait_recv()
    igo[:, cb] = (igp[rows_of(t), cb].astype(F32) + dirb[...].astype(F32) + finb[...].astype(F32)).astype(BF16)

    wait_tiles(c3, 31, bsem.at[5])
    blocks = []
    for h in range(2):
        for j in range(4):
            blocks.append(jnp.concatenate([c3[h * pieces + 4 * j + i, 0:8] for i in range(4)], axis=0))
        blocks.append(jnp.concatenate([c3[h * pieces + k, 8:10] for k in range(pieces)], axis=0))
    ct = jnp.concatenate(blocks, axis=1)
    cof[...] = lax.dot_general(linv, ct, NN, precision=HIGH, preferred_element_type=F32)

    for c in ycopies + fcopies + xcopies + zcopies + gcopies + [c_rela, c_relb, c_dira, c_dirb, c_fina, c_finb]:
        c.wait_send()
    x_swap.wait_send()
    swap_c.wait_send()
    wait_tiles(f3, 31, rsem.at[1])
    wait_tiles(f3, 31, rsem.at[2])
    wait_tiles(c3, 31, rsem.at[4])
    wait_tiles(c3, 31, rsem.at[5])


def write_out(a, b, c, ao, bo, co, sem):
    copies = [pltpu.make_async_copy(s, o, sem.at[i]) for i, (s, o) in enumerate(((a, ao), (b, bo), (c, co)))]
    for copy in copies:
        copy.start()
    for copy in copies:
        copy.wait()


def local(layer_input, pre_grad, weight_in, coeff_prev):
    rows = pre_grad.shape[0]
    scale = 1.0 / math.sqrt(rows * lax.axis_size("dp"))
    tok, width = layer_input.shape
    nt = lax.axis_size("tensor")
    hid = pre_grad.shape[1]
    share = width // nt
    half = width // 2
    nb = 8
    dma = pltpu.SemaphoreType.DMA
    vm = pltpu.VMEM
    any_spec = pl.BlockSpec(memory_space=pl.ANY)
    vmem_spec = pl.BlockSpec(memory_space=pltpu.VMEM)
    ig, basis, coeff = pl.pallas_call(
        functools.partial(kernel, scale),
        out_shape=(
            vm((tok, width), BF16),
            vm((R, share), F32),
            vm((R, hid), F32),
        ),
        in_specs=[any_spec] * 4,
        out_specs=(vmem_spec,) * 3,
        scratch_shapes=[
            vm((tok, width), BF16), vm((rows, hid), BF16), vm((R, hid), F32), vm((width, hid), BF16),
            *[vm((2, nt, tok, share // 2), BF16)] * 2,
            vm((R, rows), F32), vm((nt, R // nt, rows), F32), vm((2, nt, R // nt, rows), F32),
            vm((16, 8, 128), F32), vm((32, 8, 128), F32), vm((32, 8, 128), F32),
            vm((nt, R, rows), F32), vm((nt, R, 128), F32),
            vm((32, 10, 128), F32), vm((16, 10, 128), F32), vm((32, 10, 128), F32), vm((32, 10, 128), F32),
            vm((rows, width), BF16),
            *[vm((tok, half), BF16)] * 8,
            dma((5,)), dma((nb,)),
            *[dma((3,))] * 2, *[dma((8,))] * 2, *[dma((3,))] * 4, *[dma((7,))] * 2,
            dma((6,)), dma((6,)), dma((6,)), dma((6,)), pltpu.SemaphoreType.REGULAR,
        ],
        compiler_params=pltpu.CompilerParams(
            collective_id=0, has_side_effects=True, vmem_limit_bytes=60 * 2**20
        ),
    )(layer_input, pre_grad, weight_in, coeff_prev.T)
    ig, basis, coeff = pl.pallas_call(
        write_out,
        out_shape=tuple(jax.ShapeDtypeStruct(v.shape, v.dtype) for v in (ig, basis, coeff)),
        in_specs=[vmem_spec] * 3,
        out_specs=(any_spec,) * 3,
        scratch_shapes=[dma((3,))],
        compiler_params=pltpu.CompilerParams(vmem_limit_bytes=16 * 2**20),
    )(ig, basis, coeff)
    return ig, basis.T, coeff.T


def solution(mesh):
    return jax.shard_map(
        local,
        mesh=mesh,
        in_specs=(
            P(("dp", "tensor"), None),
            P("dp", "tensor"),
            P(None, "tensor"),
            P("tensor", None),
        ),
        out_specs=(P(("dp", "tensor"), None), P("tensor", None), P("tensor", None)),
        check_vma=False,
    )
```

```python
import functools
import math

import jax
import jax.numpy as jnp
from jax import lax
from jax.experimental import pallas as pl
from jax.experimental.pallas import tpu as pltpu
from jax.sharding import PartitionSpec as P

MESH = pl.DeviceIdType.MESH
HIGH = lax.Precision.HIGHEST
F32 = jnp.float32
BF16 = jnp.bfloat16
NN = (((1,), (0,)), ((), ()))
NT = (((1,), (1,)), ((), ()))
R = 32
NY, NZ = 4, 8


def split3(a):
    hi = a.astype(BF16)
    rest = a - hi.astype(F32)
    mid = rest.astype(BF16)
    low = (rest - mid.astype(F32)).astype(BF16)
    return jnp.concatenate([hi, mid, low], axis=0)


def fdot(pieces, b, dims):
    r = lax.dot_general(pieces, b, dims, preferred_element_type=F32)
    return r[0:R] + r[R : 2 * R] + r[2 * R : 3 * R]


def inverse_cholesky(gram):
    n = gram.shape[0]
    row = lax.broadcasted_iota(jnp.int32, (n, n), 0)
    col = lax.broadcasted_iota(jnp.int32, (n, n), 1)
    eye = jnp.where(row == col, 1.0, 0.0).astype(F32)
    m = jnp.concatenate([gram, eye], axis=1)
    below = lax.broadcasted_iota(jnp.int32, (n, 1), 0)
    diag = jnp.zeros((n, 1), F32)
    for j in range(n):
        pivot = m[j : j + 1, j : j + 1]
        column = m[:, j : j + 1]
        diag = jnp.where(below == j, pivot, diag)
        factor = jnp.where(below > j, column / pivot, 0.0)
        m = m - factor * m[j : j + 1, :]
    return m[:, n : 2 * n] / jnp.sqrt(diag)


def kernel(
    scale,
    x_ref, g_ref, w_ref, q_ref,
    igo, bas, cof,
    xv, gv, qv, wv, xh, xz, yp, yr, yf, fp, r2, f3, zr, gr, cp, hc, r4, c3,
    igp, dira, dirb, rela, relb, suma, sumb, fina, finb,
    lsem, wsem, ysem_s, ysem_r, xsem_s, xsem_r, zsem_s, zsem_r, gsem_s, gsem_r, fsem_s, fsem_r,
    rsem, bsem, isem_s, isem_r, far_sem,
):
    d = lax.axis_index("dp")
    t = lax.axis_index("tensor")
    chip = lax.div(d, 2)
    core = lax.rem(d, 2)
    cy, cz = lax.div(chip, NZ), lax.rem(chip, NZ)
    nt = 4
    tok = xv.shape[0]
    hw = xz.shape[3]
    share = 2 * hw
    half = igp.shape[1] // 2
    left, right, across = lax.rem(t + 3, nt), lax.rem(t + 1, nt), lax.rem(t + 2, nt)

    bar = pltpu.get_barrier_semaphore()

    def greet(dp, tt):
        pl.semaphore_signal(bar, inc=1, device_id=(dp, tt), device_id_type=MESH)

    def dp_index(dy, dz, dc):
        return (lax.rem(cy + dy, NY) * NZ + lax.rem(cz + dz, NZ)) * 2 + (core + dc - 2 * core * dc)

    z_line = [dp_index(0, dz, 0) for dz in (4, 3, 5, 2, 6, 1, 7)]
    group = [dp_index(dy, 0, dc) for dy in (2, 1, 3, 0) for dc in range(2) if dy or dc]
    sibling = 2 * chip + 1 - core
    for k in (2, 1, 3):
        greet(d, lax.rem(t + k, nt))
        greet(sibling, lax.rem(t + k, nt))
    for other in z_line + group:
        greet(other, t)

    loads = [
        pltpu.make_async_copy(q_ref, qv, lsem.at[0]),
        pltpu.make_async_copy(g_ref, gv, lsem.at[1]),
        pltpu.make_async_copy(x_ref, xv, lsem.at[2]),
        pltpu.make_async_copy(
            x_ref.at[:, pl.ds(pl.multiple_of(t * share + core * hw, hw), hw)], xh.at[core, t], lsem.at[3]
        ),
    ]
    for c in loads:
        c.start()
    nb = wsem.shape[0]
    wb = wv.shape[0] // nb

    def w_copy(b):
        rows = pl.ds(pl.multiple_of(b * wb, wb), wb)
        return pltpu.make_async_copy(w_ref.at[rows], wv.at[rows], wsem.at[b])

    for b in range(nb):
        w_copy(b).start()

    loads[0].wait()
    loads[1].wait()
    yp[...] = fdot(split3(qv[...]), gv[...], NT)
    ranks = R // nt

    def ranks_of(o):
        return pl.ds(pl.multiple_of(o * ranks, ranks), ranks)

    yr[t] = yp[ranks_of(t)]

    loads[2].wait()

    pl.semaphore_wait(bar, len(z_line) + len(group) + 2 * (nt - 1))

    def x_copy(to, dc, n):
        half = core + dc - 2 * core * dc
        return pltpu.make_async_remote_copy(
            src_ref=xv.at[:, pl.ds(pl.multiple_of(to * share + half * hw, hw), hw)], dst_ref=xh.at[core, t],
            send_sem=xsem_s.at[n], recv_sem=xsem_r.at[n],
            device_id=(d if dc == 0 else sibling, to), device_id_type=MESH)

    ycopies, xcopies = [], []
    for k in (2, 1, 3):
        to = lax.rem(t + k, nt)
        ycopies.append(pltpu.make_async_remote_copy(
            src_ref=yp.at[ranks_of(to)], dst_ref=yr.at[t], send_sem=ysem_s.at[k - 1], recv_sem=ysem_r.at[k - 1],
            device_id=(d, to), device_id_type=MESH))
        for dc in range(2):
            xcopies.append(x_copy(to, dc, 2 * k - 2 + dc))
    xcopies.append(x_copy(t, 1, 6))
    for c in ycopies:
        c.start()
    for c in xcopies:
        c.start()

    for other in z_line:
        pl.semaphore_signal(far_sem, inc=1, device_id=(other, t), device_id_type=MESH)

    def ig_block(b, carry):
        w_copy(b).wait()
        rows = pl.ds(pl.multiple_of(b * wb, wb), wb)
        igp[:, rows] = lax.dot_general(gv[...], wv[rows, :], NT, preferred_element_type=F32).astype(BF16)
        return carry

    lax.fori_loop(0, nb // 2, ig_block, 0)
    for c in ycopies:
        c.wait_recv()
    yf[core, t] = (yr[0] + yr[1]) + (yr[2] + yr[3])
    fcopies = []
    for k in (2, 1, 3, 0):
        for dc in range(2):
            if k or dc:
                fcopies.append(pltpu.make_async_remote_copy(
                    src_ref=yf.at[core, t], dst_ref=yf.at[core, t],
                    send_sem=fsem_s.at[2 * k + dc - 1], recv_sem=fsem_r.at[2 * k + dc - 1],
                    device_id=(d if dc == 0 else sibling, lax.rem(t + k, nt)), device_id_type=MESH))
    for c in fcopies:
        c.start()
    lax.fori_loop(nb // 2, nb, ig_block, 0)

    for c in fcopies:
        c.wait_recv()
    yt = jnp.concatenate([yf[g].reshape(R, nt * tok) for g in range(2)], axis=1)
    for c in xcopies:
        c.wait_recv()
    loads[3].wait()

    def wait_tiles(ref, n, sem):
        view = ref.at[pl.ds(0, n)]
        pltpu.make_async_copy(view, view, sem).wait()

    def tile_copy(src, dst, dp, s, r):
        return pltpu.make_async_remote_copy(
            src_ref=src, dst_ref=dst, send_sem=rsem.at[s], recv_sem=bsem.at[r],
            device_id=(dp, t), device_id_type=MESH)

    oys = [lax.rem(cy + dy, NY) for dy in range(NY)]
    ozs = [lax.rem(cz + dz, NZ) for dz in range(NZ)]
    dev_y = [oy * (2 * NZ) + core for oy in oys]
    dev_z = [2 * oz for oz in ozs]
    tile_y = [lax.rem(oy, 2) * NZ for oy in oys]
    turn_y = [lax.div(oy, 2) for oy in oys]
    turn_z = [lax.rem(oz + NZ // 2, NZ) - oz for oz in ozs]

    def device(dy, dz):
        return dev_y[dy] + dev_z[dz]

    def tile_of(dy, dz):
        return tile_y[dy] + ozs[dz] + turn_y[dy] * turn_z[dz]

    far_first = [(dy, dz) for dz in (4, 3, 5, 2, 6, 1, 7, 0) for dy in (2, 1, 3, 0) if dy or dz]

    served = [(dy, dz) for dz in (2, 6, 1, 7, 0) for dy in (2, 1, 3, 0)
              if dz in (1, 7) or (dz == 2 and dy != 2) or (dz == 6 and dy == 0) or (dz == 0 and dy)]

    last = NY * NZ - 1
    pieces = fp.shape[0]
    other_core = 1 - 2 * core
    own_tile = tile_of(0, 0)

    part = fdot(split3(yt), xh[...].reshape(2 * nt * tok, hw), NN) * scale
    for k in range(pieces):
        i, j = k % 4, k // 4
        fp[k] = part[8 * i : 8 * i + 8, 128 * j : 128 * j + 128]

    def half_of(h):
        return pl.ds(h * pieces, pieces)

    pl.semaphore_wait(far_sem, len(z_line))
    base = core * pieces
    for dy, dz in far_first:
        tile_copy(fp.at[tile_of(dy, dz)], r2.at[chip], device(dy, dz), 1, 1).start()
    mine = base + own_tile
    r2[chip] = fp[own_tile]

    x_swap = pltpu.make_async_remote_copy(
        src_ref=xh.at[1 - core], dst_ref=xz.at[core], send_sem=xsem_s.at[7], recv_sem=xsem_r.at[7],
        device_id=(sibling, t), device_id_type=MESH)
    x_swap.start()
    x_keep = pltpu.make_async_copy(xh.at[core], xz.at[core], lsem.at[4])
    x_keep.start()

    def rows_of(o):
        return pl.ds(pl.multiple_of(o * tok, tok), tok)

    def ig_copy(n, src, dst, to):
        return pltpu.make_async_remote_copy(
            src_ref=src, dst_ref=dst, send_sem=isem_s.at[n], recv_sem=isem_r.at[n],
            device_id=(d, to), device_id_type=MESH)

    ca, cb = pl.ds(0, half), pl.ds(half, half)
    c_rela = ig_copy(0, igp.at[rows_of(across), ca], rela, left)
    c_relb = ig_copy(1, igp.at[rows_of(across), cb], relb, right)
    c_dira = ig_copy(2, igp.at[rows_of(right), ca], dira, right)
    c_dirb = ig_copy(3, igp.at[rows_of(left), cb], dirb, left)
    for c in (c_rela, c_relb, c_dira, c_dirb):
        c.start()

    wait_tiles(r2, last, bsem.at[1])
    f3[mine] = jnp.sum(r2[...], axis=0)
    def broadcast(ref, tile, s, r):
        for dy, dz in served:
            for other in (device(dy, dz), device(dy, dz) + other_core):
                tile_copy(ref.at[tile], ref.at[tile], other, s, r).start()
        tile_copy(ref.at[tile], ref.at[tile], sibling, s, r).start()

    broadcast(f3, mine, 2, 2)
    wait_tiles(f3, 31, bsem.at[2])

    def columns(h):
        return jnp.concatenate(
            [jnp.concatenate([f3[h * pieces + 4 * j + i] for j in range(hw // 128)], axis=1) for i in range(4)], axis=0
        )

    x_keep.wait()
    x_swap.wait_recv()
    halves = [columns(0), columns(1)]
    ft = jnp.concatenate(halves, axis=1)
    z_parts = [fdot(split3(halves[h]), xz[h].reshape(nt * tok, hw), NT) for h in range(2)]

    zr[t] = (z_parts[0] + z_parts[1]) * scale
    zcopies, gcopies = [], []
    for k in (2, 1, 3):
        zcopies.append(pltpu.make_async_remote_copy(
            src_ref=zr.at[t], dst_ref=zr.at[t], send_sem=zsem_s.at[k - 1], recv_sem=zsem_r.at[k - 1],
            device_id=(d, lax.rem(t + k, nt)), device_id_type=MESH))
    for c in zcopies:
        c.start()
    gr[t, :, 0:R] = lax.dot_general(ft, ft, NT, precision=HIGH, preferred_element_type=F32)
    for k in (2, 1, 3):
        gcopies.append(pltpu.make_async_remote_copy(
            src_ref=gr.at[t], dst_ref=gr.at[t], send_sem=gsem_s.at[k - 1], recv_sem=gsem_r.at[k - 1],
            device_id=(d, lax.rem(t + k, nt)), device_id_type=MESH))
    for c in gcopies:
        c.start()
    for c in zcopies:
        c.wait_recv()
    zt = (zr[0] + zr[1]) + (zr[2] + zr[3])

    zs = split3(zt)
    width_c = gv.shape[1] // 2
    edge_c = width_c - 128

    def coeff_half(h):
        columns = pl.ds(pl.multiple_of(h * width_c, 128), width_c)
        part = fdot(zs, gv[:, columns], NN)
        for k in range(pieces):
            i, j = k % 4, k // 4
            cp[h * pieces + k, 0:8] = part[8 * i : 8 * i + 8, 128 * j : 128 * j + 128]
            cp[h * pieces + k, 8:10] = part[2 * k : 2 * k + 2, edge_c:width_c]

    coeff_half(1 - core)
    swap_c = tile_copy(cp.at[half_of(1 - core)], hc, sibling, 3, 3)
    swap_c.start()
    coeff_half(core)
    swap_c.wait_recv()
    cp[half_of(core)] = cp[half_of(core)] + hc[...]
    for dy, dz in far_first:
        tile_copy(cp.at[base + tile_of(dy, dz)], r4.at[chip], device(dy, dz), 4, 4).start()
    r4[chip] = cp[mine]

    c_rela.wait_recv()
    suma[...] = (rela[...].astype(F32) + igp[rows_of(left), ca].astype(F32)).astype(BF16)
    c_fina = ig_copy(4, suma, fina, left)
    c_fina.start()
    c_relb.wait_recv()
    sumb[...] = (relb[...].astype(F32) + igp[rows_of(right), cb].astype(F32)).astype(BF16)
    c_finb = ig_copy(5, sumb, finb, right)
    c_finb.start()

    for c in gcopies:
        c.wait_recv()
    gs = slice(0, R)
    gram = (gr[0, :, gs] + gr[1, :, gs]) + (gr[2, :, gs] + gr[3, :, gs])
    linv = inverse_cholesky(gram)
    bas[...] = lax.dot_general(linv, ft, NN, precision=HIGH, preferred_element_type=F32)

    wait_tiles(r4, last, bsem.at[4])
    c3[mine] = jnp.sum(r4[...], axis=0)
    broadcast(c3, mine, 5, 5)

    c_dira.wait_recv()
    c_fina.wait_recv()
    igo[:, ca] = (igp[rows_of(t), ca].astype(F32) + dira[...].astype(F32) + fina[...].astype(F32)).astype(BF16)
    c_dirb.wait_recv()
    c_finb.wait_recv()
    igo[:, cb] = (igp[rows_of(t), cb].astype(F32) + dirb[...].astype(F32) + finb[...].astype(F32)).astype(BF16)

    wait_tiles(c3, 31, bsem.at[5])
    blocks = []
    for h in range(2):
        for j in range(4):
            blocks.append(jnp.concatenate([c3[h * pieces + 4 * j + i, 0:8] for i in range(4)], axis=0))
        blocks.append(jnp.concatenate([c3[h * pieces + k, 8:10] for k in range(pieces)], axis=0))
    ct = jnp.concatenate(blocks, axis=1)
    cof[...] = lax.dot_general(linv, ct, NN, precision=HIGH, preferred_element_type=F32)

    for c in ycopies + fcopies + xcopies + zcopies + gcopies + [c_rela, c_relb, c_dira, c_dirb, c_fina, c_finb]:
        c.wait_send()
    x_swap.wait_send()
    swap_c.wait_send()
    wait_tiles(f3, 31, rsem.at[1])
    wait_tiles(f3, 31, rsem.at[2])
    wait_tiles(c3, 31, rsem.at[4])
    wait_tiles(c3, 31, rsem.at[5])


def write_out(a, b, c, ao, bo, co, sem):
    copies = [pltpu.make_async_copy(s, o, sem.at[i]) for i, (s, o) in enumerate(((a, ao), (b, bo), (c, co)))]
    for copy in copies:
        copy.start()
    for copy in copies:
        copy.wait()


def local(layer_input, pre_grad, weight_in, coeff_prev):
    rows = pre_grad.shape[0]
    scale = 1.0 / math.sqrt(rows * lax.axis_size("dp"))
    tok, width = layer_input.shape
    nt = lax.axis_size("tensor")
    hid = pre_grad.shape[1]
    share = width // nt
    half = width // 2
    nb = 8
    dma = pltpu.SemaphoreType.DMA
    vm = pltpu.VMEM
    any_spec = pl.BlockSpec(memory_space=pl.ANY)
    vmem_spec = pl.BlockSpec(memory_space=pltpu.VMEM)
    ig, basis, coeff = pl.pallas_call(
        functools.partial(kernel, scale),
        out_shape=(
            vm((tok, width), BF16),
            vm((R, share), F32),
            vm((R, hid), F32),
        ),
        in_specs=[any_spec] * 4,
        out_specs=(vmem_spec,) * 3,
        scratch_shapes=[
            vm((tok, width), BF16), vm((rows, hid), BF16), vm((R, hid), F32), vm((width, hid), BF16),
            *[vm((2, nt, tok, share // 2), BF16)] * 2,
            vm((R, rows), F32), vm((nt, R // nt, rows), F32), vm((2, nt, R // nt, rows), F32),
            vm((16, 8, 128), F32), vm((32, 8, 128), F32), vm((32, 8, 128), F32),
            vm((nt, R, rows), F32), vm((nt, R, 128), F32),
            vm((32, 10, 128), F32), vm((16, 10, 128), F32), vm((32, 10, 128), F32), vm((32, 10, 128), F32),
            vm((rows, width), BF16),
            *[vm((tok, half), BF16)] * 8,
            dma((5,)), dma((nb,)),
            *[dma((3,))] * 2, *[dma((8,))] * 2, *[dma((3,))] * 4, *[dma((7,))] * 2,
            dma((6,)), dma((6,)), dma((6,)), dma((6,)), pltpu.SemaphoreType.REGULAR,
        ],
        compiler_params=pltpu.CompilerParams(
            collective_id=0, has_side_effects=True, vmem_limit_bytes=60 * 2**20
        ),
    )(layer_input, pre_grad, weight_in, coeff_prev.T)
    ig, basis, coeff = pl.pallas_call(
        write_out,
        out_shape=tuple(jax.ShapeDtypeStruct(v.shape, v.dtype) for v in (ig, basis, coeff)),
        in_specs=[vmem_spec] * 3,
        out_specs=(any_spec,) * 3,
        scratch_shapes=[dma((3,))],
        compiler_params=pltpu.CompilerParams(vmem_limit_bytes=16 * 2**20),
    )(ig, basis, coeff)
    return ig, basis.T, coeff.T


def solution(mesh):
    return jax.shard_map(
        local,
        mesh=mesh,
        in_specs=(
            P(("dp", "tensor"), None),
            P("dp", "tensor"),
            P(None, "tensor"),
            P("tensor", None),
        ),
        out_specs=(P(("dp", "tensor"), None), P("tensor", None), P("tensor", None)),
        check_vma=False,
    )
```
